32 devices in a mesh: grp: 4 (over y, x), cp: 8 (over z, core).
Axes of the slice: x: 2, y: 2, z: 4, core: 2. Of those that a mesh axis runs over, the one named last changes fastest.
Arguments:
- queries: bfloat16 [4, 4096, 4096], P(None, ('grp', 'cp')), may hold values from -6 to 6, as said below
- keys: bfloat16 [4, 4096, 1024], P(None, ('grp', 'cp')), may hold values from -6 to 6, as said below
- values: bfloat16 [4, 4096, 1024], P(None, ('grp', 'cp')), may hold values from -6 to 6
- doc_lengths: int32 [4, 16], replicated, may hold values from 1 to 1024, 4096 in all within a row
Outputs:
- attended: bfloat16 [4, 4096, 4096], P(None, ('grp', 'cp'))
The draws below stay inside these ranges and needn't reach their ends.
Inputs may be any that keep to these rules, and one draw needn't show every extreme that they name: `doc_lengths`: each row holds the lengths of 16 documents that fill the stream's 4096 tokens exactly; the longest is exactly 1024 tokens. `queries`: entries of order one. `keys`: entries of order one.
All inputs are finite; a program needn't handle non-finite values.
Results may differ from the reference program's by a relative error of at most 0.0038.
Values may be sent and summed in bfloat16 or wider, within the bound.
A program may use at most 128 MiB of HBM per device.

```python
import math
import jax
import jax.numpy as jnp
import numpy as np
from jax import lax

QUERY_HEADS = 32
KEY_VALUE_HEADS = 8
HEAD_WIDTH = 128
DOCS = 16
STREAM_COUNT = 4
STREAM_TOKENS = 4096
KVD = 1024
MOST = 1024


def draw_queries(key, part):
    array_extent = (STREAM_COUNT, STREAM_TOKENS, QUERY_HEADS * HEAD_WIDTH)
    result = jnp.clip(jax.random.normal(jax.random.fold_in(key, 1), array_extent, jnp.float32), -6.0, 6.0)
    return result.astype(jnp.bfloat16)


def draw_keys(key, part):
    array_extent = (STREAM_COUNT, STREAM_TOKENS, KEY_VALUE_HEADS * HEAD_WIDTH)
    result = jnp.clip(jax.random.normal(jax.random.fold_in(key, 2), array_extent, jnp.float32), -6.0, 6.0)
    return result.astype(jnp.bfloat16)


def shard_levels(stream_key, extent, shards, smallest, top_value):
    level = 1.0
    for axis_at, parts in shards:
        steps = jax.random.uniform(jax.random.fold_in(jax.random.fold_in(stream_key, 6), axis_at), (parts,), jnp.float32, smallest / len(shards), top_value / len(shards))
        level = level * jnp.repeat(jnp.exp(steps), extent[axis_at] // parts).reshape((-1,) + (1,) * (len(extent) - 1 - axis_at))
    return level


def length_profile(number_of, total, bound, slope):
    weights = [(1 << 20) // math.isqrt(standing ** slope) + 1 for standing in range(2, number_of + 1)]
    surplus, counts = total - bound - (number_of - 1), [1] * (number_of - 1)
    while surplus > 0:
        candidates = [i for i in range(number_of - 1) if counts[i] < bound]
        whole, remaining = sum([weights[i] for i in candidates]), surplus
        for i in candidates:
            more = min(bound - counts[i], max(1, remaining * weights[i] // whole), surplus)
            counts[i] = counts[i] + more
            surplus = surplus - more
    return np.array([bound] + counts)


def uneven_parts(rng, amount, total, bound, skew):
    if amount == 2:
        one = jax.random.randint(rng, (), max(1, total - bound), min(bound, total - 1) + 1)
        return jnp.stack([one, total - one])
    sizes = jnp.asarray(length_profile(amount, total, bound, skew), jnp.int32)
    twos = (amount - 1) // 2
    giver, receiver = sizes[1:1 + 2 * twos:2], sizes[2:2 + 2 * twos:2]
    slack = jnp.minimum(giver - 1, bound - receiver)
    passed = jax.random.randint(jax.random.fold_in(rng, 1), (twos,), 0, 1 << 20) % (slack + 1)
    sizes = sizes.at[1:1 + 2 * twos:2].set(giver - passed).at[2:2 + 2 * twos:2].set(receiver + passed)
    return sizes[jax.random.permutation(jax.random.fold_in(rng, 2), amount)]


def gaussian(own_key, dims, deviation, most, shards=(), held_as=jnp.bfloat16):
    entries = deviation * jax.random.normal(own_key, dims, jnp.float32)
    if shards:
        entries = entries * shard_levels(own_key, dims, shards, -0.22, 0.18)
    return jnp.clip(entries, -most, most).astype(held_as)


def setup_inputs(seed: int = 0) -> dict:
    key_list = jax.random.split(jax.random.key(seed), 5)
    return {
        "queries": draw_queries(jax.random.fold_in(key_list[4], 71), 0),
        "keys": draw_keys(jax.random.fold_in(key_list[4], 71), 0),
        "values": gaussian(key_list[2], (STREAM_COUNT, STREAM_TOKENS, KVD), 1.0, 6.0, ((1, 32),)),
        "doc_lengths": jax.vmap(lambda own: uneven_parts(own, DOCS, STREAM_TOKENS, MOST, 2))(jax.random.split(key_list[3], STREAM_COUNT)).reshape((STREAM_COUNT, DOCS)).astype(jnp.int32),
    }


def doc_index(lengths_row, positions):
    ends = jnp.cumsum(lengths_row)
    return jnp.sum((positions[:, None] >= ends[None, :]).astype(jnp.int32), axis=1)


def reference(queries, keys, values, doc_lengths):
    group_count = QUERY_HEADS // KEY_VALUE_HEADS
    scale = HEAD_WIDTH ** -0.5
    query_block_rows = min(256, STREAM_TOKENS)
    visible_span = min(MOST + query_block_rows, STREAM_TOKENS)

    def one_stream(bundle):
        query_rows, key_rows, value_rows, lengths_row = bundle
        positions = jnp.arange(STREAM_TOKENS, dtype=jnp.int32)
        docs = doc_index(lengths_row, positions)

        def one_block(begin):
            first = jnp.clip(begin + query_block_rows - visible_span, 0, STREAM_TOKENS - visible_span).astype(jnp.int32)
            key_portion = lax.dynamic_slice_in_dim(key_rows, first, visible_span, 0)
            value_portion = lax.dynamic_slice_in_dim(value_rows, first, visible_span, 0)
            heads_of_key = key_portion.reshape(visible_span, KEY_VALUE_HEADS, HEAD_WIDTH).astype(jnp.float32)
            heads_of_value = value_portion.reshape(visible_span, KEY_VALUE_HEADS, HEAD_WIDTH).astype(jnp.float32)
            key_pos = lax.dynamic_slice_in_dim(positions, first, visible_span, 0)
            key_doc = lax.dynamic_slice_in_dim(docs, first, visible_span, 0)
            block_of_queries = lax.dynamic_slice_in_dim(query_rows, begin, query_block_rows, 0)
            block_of_queries = block_of_queries.reshape(query_block_rows, KEY_VALUE_HEADS, group_count, HEAD_WIDTH).astype(jnp.float32)
            query_pos = begin + jnp.arange(query_block_rows, dtype=jnp.int32)
            query_doc = lax.dynamic_slice_in_dim(docs, begin, query_block_rows, 0)
            allowed = (key_pos[None, :] <= query_pos[:, None]) & (key_doc[None, :] == query_doc[:, None])
            scores = jnp.einsum("qhgd,khd->hgqk", block_of_queries, heads_of_key) * scale
            scores = jnp.where(allowed, scores, -1e30)
            largest = jnp.max(scores, axis=-1, keepdims=True)
            probs = jnp.where(allowed, jnp.exp(scores - largest), 0.0)
            total = jnp.sum(probs, axis=-1)
            weights = lax.optimization_barrier(probs.astype(jnp.bfloat16)).astype(jnp.float32)
            summed = jnp.einsum("hgqk,khd->hgqd", weights, heads_of_value)
            result = summed / total[..., None]
            return result.transpose(2, 0, 1, 3).reshape(query_block_rows, QUERY_HEADS * HEAD_WIDTH).astype(jnp.bfloat16)

        starts = jnp.arange(STREAM_TOKENS // query_block_rows, dtype=jnp.int32) * query_block_rows
        return lax.map(one_block, starts).reshape(STREAM_TOKENS, QUERY_HEADS * HEAD_WIDTH)

    return lax.map(one_stream, (queries, keys, values, doc_lengths))
```

```python
import functools

import jax
import jax.numpy as jnp
from jax import lax
from jax.experimental import pallas as pl
from jax.experimental.pallas import tpu as pltpu
from jax.sharding import PartitionSpec as P

MESH = pl.DeviceIdType.MESH
PARTS = 2
WINDOW_BYTES = 40 * 2**20

QUERY_HEADS = 32
KEY_VALUE_HEADS = 8
HEAD_WIDTH = 128
NEGATIVE = -1e30
LOG2_E = 1.4426950408889634


def window_kernel(
    n_grp, n_cp, streams, q_ref, k_ref, v_ref, len_ref, o_ref, kv, bias, local_sem, send_sem, recv_sem
):
    grp, cp = lax.axis_index("grp"), lax.axis_index("cp")
    z, core = cp // 2, cp % 2
    nz = n_cp // 2
    chunks = streams * PARTS
    rows = k_ref.shape[1]
    part = k_ref.shape[2] // PARTS
    heads = part // HEAD_WIDTH
    group = QUERY_HEADS // KEY_VALUE_HEADS
    partner = (grp, z * 2 + 1 - core)
    up = (grp, cp + 2)
    down = (grp, cp - 2)
    next_line = ((grp + 1) % n_grp, cp)
    prev_line = ((grp + n_grp - 1) % n_grp, cp)
    fwd_row, hop_row, bwd_row, mate_row = 0, nz - 1, nz - 2, 2 * nz - 1

    def local(ch, which):
        source = (k_ref, v_ref)[which]
        cols = pl.ds(pl.multiple_of((ch % PARTS) * part, part), part)
        return pltpu.make_async_copy(
            source.at[ch // PARTS, :, cols],
            kv.at[0, ch, :, pl.ds(which * part, part)],
            local_sem.at[which, ch],
        )

    def remote(source, target, ch, row, device):
        return pltpu.make_async_remote_copy(
            src_ref=kv.at[source, ch],
            dst_ref=kv.at[target, ch],
            send_sem=send_sem.at[row, ch],
            recv_sem=recv_sem.at[target, ch],
            device_id=device,
            device_id_type=MESH,
        )

    def arrived(slot, ch):
        remote(slot, slot, ch, 0, partner).wait_recv()

    @pl.loop(0, chunks)
    def _(ch):
        local(ch, 0).start()
        local(ch, 1).start()

    barrier = pltpu.get_barrier_semaphore()

    def greet(device):
        pl.semaphore_signal(barrier, inc=1, device_id=device, device_id_type=MESH)

    greet(partner)
    greet(next_line)
    greet(prev_line)

    @pl.when(z < nz - 1)
    def _():
        greet(up)

    @pl.when(z > 0)
    def _():
        greet(down)

    at_end = (z == 0) | (z == nz - 1)
    pl.semaphore_wait(barrier, jnp.where(at_end, 4, 5))

    def to_partner(d, ch):
        if d < nz:

            @pl.when(core == 0)
            def _():
                remote(2 * d, 2 * d + 1, ch, mate_row + d, partner).start()

        if d > 0:

            @pl.when(core == 1)
            def _():
                remote(2 * d, 2 * d - 1, ch, mate_row + d, partner).start()

    def attend(ch):
        stream, piece = ch // PARTS, ch % PARTS
        base = (grp * n_cp + cp) * rows
        row = lax.broadcasted_iota(jnp.int32, (rows, rows), 0)
        lane = lax.broadcasted_iota(jnp.int32, (rows, rows), 1)
        first = jnp.zeros((rows, rows), jnp.int32)
        end = jnp.int32(0)
        for doc in range(len_ref.shape[1]):
            end = end + len_ref[stream, doc]
            first = jnp.maximum(first, jnp.where(row + base >= end, end, 0))
        for r in range(n_cp + 1):
            allowed = lane + (base - r * rows) >= first
            if r == 0:
                allowed = allowed & (lane <= row)
            bias[:, r * rows : (r + 1) * rows] = jnp.where(allowed, 0.0, NEGATIVE)

        @pl.loop(0, heads)
        def _(head):
            k_cols = pl.ds(pl.multiple_of(head * HEAD_WIDTH, HEAD_WIDTH), HEAD_WIDTH)
            v_cols = pl.ds(pl.multiple_of(part + head * HEAD_WIDTH, HEAD_WIDTH), HEAD_WIDTH)
            k_all = jnp.concatenate([kv[r, ch, :, k_cols] for r in range(n_cp + 1)], axis=0)
            v_all = jnp.concatenate([kv[r, ch, :, v_cols] for r in range(n_cp + 1)], axis=0)
            for j in range(group):
                at = ((piece * heads + head) * group + j) * HEAD_WIDTH
                q_cols = pl.ds(pl.multiple_of(at, HEAD_WIDTH), HEAD_WIDTH)
                scores = lax.dot_general(
                    q_ref[stream, :, q_cols],
                    k_all,
                    (((1,), (1,)), ((), ())),
                    preferred_element_type=jnp.float32,
                )
                scores = scores + bias[...]
                largest = jnp.max(scores, axis=1, keepdims=True)
                probs = jnp.exp2((scores - largest) * (HEAD_WIDTH**-0.5 * LOG2_E))
                total = jnp.sum(probs, axis=1, keepdims=True)
                summed = jnp.dot(
                    probs.astype(jnp.bfloat16), v_all, preferred_element_type=jnp.float32
                )
                o_ref[stream, :, q_cols] = (summed / total).astype(o_ref.dtype)

    @pl.loop(0, chunks + nz)
    def _(t):
        @pl.when(t < chunks)
        def _():
            local(t, 0).wait()
            local(t, 1).wait()
            remote(0, 2 * nz, t, hop_row, next_line).start()

            @pl.when(z < nz - 1)
            def _():
                remote(0, 2, t, fwd_row, up).start()

            to_partner(0, t)

        for d in range(nz, 0, -1):
            ch = t - (nz + 1 - d)

            @pl.when((ch >= 0) & (ch < chunks) & (z < d))
            def _():
                arrived(2 * d, ch)
                if d > 1:

                    @pl.when(z > 0)
                    def _():
                        remote(2 * d, 2 * d - 2, ch, bwd_row + d, down).start()

                to_partner(d, ch)

        for d in range(1, nz):
            ch = t - d

            @pl.when((ch >= 0) & (ch < chunks) & (z >= d))
            def _():
                arrived(2 * d, ch)
                if d < nz - 1:

                    @pl.when(z < nz - 1)
                    def _():
                        remote(2 * d, 2 * d + 2, ch, fwd_row + d, up).start()

                to_partner(d, ch)

        @pl.when(t >= nz)
        def _():
            ch = t - nz
            for d in range(nz):
                arrived(2 * d + 1, ch)
            attend(ch)

    @pl.loop(0, chunks)
    def _(ch):
        def sent(row):
            remote(0, 1, ch, row, partner).wait_send()

        sent(hop_row)
        for d in range(nz - 1):

            @pl.when((z >= d) & (z < nz - 1))
            def _():
                sent(fwd_row + d)

        for d in range(2, nz + 1):

            @pl.when((z < d) & (z > 0))
            def _():
                sent(bwd_row + d)

        for d in range(nz + 1):
            if d == 0:

                @pl.when(core == 0)
                def _():
                    sent(mate_row)

            elif d == nz:

                @pl.when(core == 1)
                def _():
                    sent(mate_row + nz)

            else:
                sent(mate_row + d)


def by_window(n_grp, n_cp, queries, keys, values, doc_lengths):
    streams, rows, _ = queries.shape
    chunks = streams * PARTS
    width = 2 * keys.shape[2] // PARTS
    window = (n_cp + 1) * rows
    nz = n_cp // 2
    pairs = streams * QUERY_HEADS * rows * window
    return pl.pallas_call(
        functools.partial(window_kernel, n_grp, n_cp, streams),
        out_shape=jax.ShapeDtypeStruct(queries.shape, queries.dtype),
        in_specs=[
            pl.BlockSpec(memory_space=pltpu.VMEM),
            pl.BlockSpec(memory_space=pl.ANY),
            pl.BlockSpec(memory_space=pl.ANY),
            pl.BlockSpec(memory_space=pltpu.SMEM),
        ],
        out_specs=pl.BlockSpec(memory_space=pltpu.VMEM),
        scratch_shapes=[
            pltpu.VMEM((n_cp + 1, chunks, rows, width), keys.dtype),
            pltpu.VMEM((rows, window), jnp.float32),
            pltpu.SemaphoreType.DMA((2, chunks)),
            pltpu.SemaphoreType.DMA((3 * nz, chunks)),
            pltpu.SemaphoreType.DMA((n_cp + 1, chunks)),
        ],
        cost_estimate=pl.CostEstimate(
            flops=4 * pairs * HEAD_WIDTH, bytes_accessed=5 * queries.size, transcendentals=pairs
        ),
        compiler_params=pltpu.CompilerParams(
            collective_id=0, has_side_effects=True, vmem_limit_bytes=56 * 2**20
        ),
        name="window_attention",
    )(queries, keys, values, doc_lengths)


def window_fits(n_grp, n_cp, queries, keys):
    line = 2 * keys.shape[0] * keys.shape[1] // n_grp * keys.shape[2] * keys.dtype.itemsize
    return n_cp % 2 == 0 and n_cp >= 4 and n_grp >= 3 and line <= WINDOW_BYTES


def doc_of(positions, ends):
    return jnp.sum((positions[:, None] >= ends[None, :]).astype(jnp.int32), axis=1)


def doc_first(positions, ends):
    return jnp.max(jnp.where(ends[None, :] <= positions[:, None], ends[None, :], 0), axis=1)


def absorb(state, scores, allowed, value_portion):
    running_max, running_sum, running_acc = state
    scores = jnp.where(allowed, scores, NEGATIVE)
    new_max = jnp.maximum(running_max, jnp.max(scores, axis=-1))
    factor = jnp.exp(running_max - new_max)
    probs = jnp.where(allowed, jnp.exp(scores - new_max[..., None]), 0.0)
    new_sum = running_sum * factor + jnp.sum(probs, axis=-1)
    product = jnp.einsum(
        "hqk,khd->hqd",
        probs.astype(jnp.bfloat16),
        value_portion,
        preferred_element_type=jnp.float32,
    )
    return (new_max, new_sum, running_acc * factor[..., None] + product)


def attend_stream(query_seq, key_seq, value_seq, ends):
    stream_len = query_seq.shape[0]
    items = query_seq.shape[1]
    scale = HEAD_WIDTH ** (-0.5)
    positions = jnp.arange(stream_len, dtype=jnp.int32)
    all_docs = doc_of(positions, ends)
    all_firsts = doc_first(positions, ends)
    span = min(512, stream_len)
    spans = stream_len // span

    def query_span(number):
        begin = number * span
        query_tile = lax.dynamic_slice_in_dim(query_seq, begin, span, 0)
        query_pos = lax.dynamic_slice_in_dim(positions, begin, span, 0)
        query_doc = lax.dynamic_slice_in_dim(all_docs, begin, span, 0)
        first_span = lax.dynamic_index_in_dim(all_firsts, begin, 0, keepdims=False) // span

        def key_span(other, state):
            offset = other * span
            key_tile = lax.dynamic_slice_in_dim(key_seq, offset, span, 0)
            value_tile = lax.dynamic_slice_in_dim(value_seq, offset, span, 0)
            key_pos = lax.dynamic_slice_in_dim(positions, offset, span, 0)
            key_doc = lax.dynamic_slice_in_dim(all_docs, offset, span, 0)
            allowed = (key_pos[None, :] <= query_pos[:, None]) & (
                key_doc[None, :] == query_doc[:, None]
            )
            scores = (
                jnp.einsum("qhd,khd->hqk", query_tile, key_tile, preferred_element_type=jnp.float32)
                * scale
            )
            return absorb(state, scores, allowed, value_tile)

        start_state = (
            jnp.full((items, span), NEGATIVE, jnp.float32),
            jnp.zeros((items, span), jnp.float32),
            jnp.zeros((items, span, HEAD_WIDTH), jnp.float32),
        )
        final_max, final_sum, final_acc = lax.fori_loop(
            first_span, number + 1, key_span, start_state
        )
        return (final_acc / final_sum[..., None]).transpose(1, 0, 2).astype(jnp.bfloat16)

    tiles = lax.map(query_span, jnp.arange(spans, dtype=jnp.int32))
    return tiles.reshape(stream_len, items, HEAD_WIDTH)


def on_device(queries, keys, values, doc_lengths):
    n_ranks = lax.axis_size("cp")
    n_streams = queries.shape[0]
    rows_per = queries.shape[1]
    group_count = QUERY_HEADS // KEY_VALUE_HEADS
    per_rank = QUERY_HEADS // n_ranks
    stream_id = lax.axis_index("grp")
    lengths_row = lax.dynamic_index_in_dim(doc_lengths, stream_id, 0, keepdims=False)
    ends = jnp.cumsum(lengths_row)

    def by_heads(array):
        shaped = array.reshape(n_streams, rows_per, n_ranks, per_rank, HEAD_WIDTH)
        return shaped.transpose(0, 2, 1, 3, 4).reshape(
            n_streams * n_ranks, rows_per, per_rank, HEAD_WIDTH
        )

    key_wide = jnp.repeat(
        keys.reshape(n_streams, rows_per, KEY_VALUE_HEADS, HEAD_WIDTH), group_count, axis=2
    )
    value_wide = jnp.repeat(
        values.reshape(n_streams, rows_per, KEY_VALUE_HEADS, HEAD_WIDTH), group_count, axis=2
    )
    query_split = by_heads(queries)
    key_divided_rows = by_heads(key_wide)
    value_divided_rows = by_heads(value_wide)
    query_part = lax.all_to_all(query_split, ("grp", "cp"), split_axis=0, concat_axis=1, tiled=True)
    key_portion = lax.all_to_all(
        key_divided_rows, ("grp", "cp"), split_axis=0, concat_axis=1, tiled=True
    )
    value_portion = lax.all_to_all(
        value_divided_rows, ("grp", "cp"), split_axis=0, concat_axis=1, tiled=True
    )
    outcome = attend_stream(query_part[0], key_portion[0], value_portion[0], ends)
    head_output = outcome[None]
    returned = lax.all_to_all(head_output, ("grp", "cp"), split_axis=1, concat_axis=0, tiled=True)
    shaped = returned.reshape(n_streams, n_ranks, rows_per, per_rank, HEAD_WIDTH).transpose(
        0, 2, 1, 3, 4
    )
    return shaped.reshape(n_streams, rows_per, QUERY_HEADS * HEAD_WIDTH)


def solution(mesh):
    n_grp, n_cp = mesh.shape["grp"], mesh.shape["cp"]
    placed = (
        P(None, ("grp", "cp"), None),
        P(None, ("grp", "cp"), None),
        P(None, ("grp", "cp"), None),
        P(),
    )

    def run(queries, keys, values, doc_lengths):
        if window_fits(n_grp, n_cp, queries, keys):
            plan = functools.partial(by_window, n_grp, n_cp)
        else:
            plan = on_device
        return jax.shard_map(
            plan,
            mesh=mesh,
            in_specs=placed,
            out_specs=P(None, ("grp", "cp"), None),
            check_vma=False,
        )(queries, keys, values, doc_lengths)

    return run
```

```python
import functools

import jax
import jax.numpy as jnp
from jax import lax
from jax.experimental import pallas as pl
from jax.experimental.pallas import tpu as pltpu
from jax.sharding import PartitionSpec as P

MESH = pl.DeviceIdType.MESH
PARTS = 4
WINDOW_BYTES = 40 * 2**20

QUERY_HEADS = 32
KEY_VALUE_HEADS = 8
HEAD_WIDTH = 128
NEGATIVE = -1e30
LOG2_E = 1.4426950408889634


def window_kernel(
    n_grp,
    n_cp,
    streams,
    q_ref,
    k_ref,
    v_ref,
    len_ref,
    o_ref,
    kv,
    q_buf,
    o_buf,
    bias,
    local_sem,
    send_sem,
    recv_sem,
):
    grp, cp = lax.axis_index("grp"), lax.axis_index("cp")
    z, core = cp // 2, cp % 2
    nz = n_cp // 2
    chunks = streams * PARTS
    rows = k_ref.shape[1]
    part = k_ref.shape[2] // PARTS
    heads = part // HEAD_WIDTH
    group = QUERY_HEADS // KEY_VALUE_HEADS
    wide = part * group
    partner = (grp, z * 2 + 1 - core)
    up = (grp, cp + 2)
    down = (grp, cp - 2)
    next_line = ((grp + 1) % n_grp, cp)
    prev_line = ((grp + n_grp - 1) % n_grp, cp)
    fwd_row, hop_row, bwd_row, mate_row = 0, nz - 1, nz - 2, 2 * nz - 1

    def local(ch, which):
        source = (k_ref, v_ref)[which]
        cols = pl.ds(pl.multiple_of((ch % PARTS) * part, part), part)
        return pltpu.make_async_copy(
            source.at[ch // PARTS, :, cols],
            kv.at[0, ch, :, pl.ds(which * part, part)],
            local_sem.at[which, ch],
        )

    def own_columns(ch):
        return ch // PARTS, slice(None), pl.ds(pl.multiple_of((ch % PARTS) * wide, wide), wide)

    def query_copy(ch):
        at = own_columns(ch)
        return pltpu.make_async_copy(q_ref.at[at], q_buf.at[at], local_sem.at[2, ch])

    def result_copy(ch):
        at = own_columns(ch)
        return pltpu.make_async_copy(o_buf.at[at], o_ref.at[at], local_sem.at[3, ch])

    def remote(source, target, ch, row, device):
        return pltpu.make_async_remote_copy(
            src_ref=kv.at[source, ch],
            dst_ref=kv.at[target, ch],
            send_sem=send_sem.at[row, ch],
            recv_sem=recv_sem.at[target, ch],
            device_id=device,
            device_id_type=MESH,
        )

    def arrived(slot, ch):
        remote(slot, slot, ch, 0, partner).wait_recv()

    @pl.loop(0, chunks)
    def _(ch):
        local(ch, 0).start()
        local(ch, 1).start()

    @pl.loop(0, chunks)
    def _(ch):
        query_copy(ch).start()

    barrier = pltpu.get_barrier_semaphore()

    def greet(device):
        pl.semaphore_signal(barrier, inc=1, device_id=device, device_id_type=MESH)

    greet(partner)
    greet(next_line)
    greet(prev_line)

    @pl.when(z < nz - 1)
    def _():
        greet(up)

    @pl.when(z > 0)
    def _():
        greet(down)

    at_end = (z == 0) | (z == nz - 1)
    pl.semaphore_wait(barrier, jnp.where(at_end, 4, 5))

    def to_partner(d, ch):
        if d < nz:

            @pl.when(core == 0)
            def _():
                remote(2 * d, 2 * d + 1, ch, mate_row + d, partner).start()

        if d > 0:

            @pl.when(core == 1)
            def _():
                remote(2 * d, 2 * d - 1, ch, mate_row + d, partner).start()

    def attend(ch):
        stream, piece = ch // PARTS, ch % PARTS
        base = (grp * n_cp + cp) * rows
        row = lax.broadcasted_iota(jnp.int32, (rows, rows), 0)
        lane = lax.broadcasted_iota(jnp.int32, (rows, rows), 1)
        first = jnp.zeros((rows, rows), jnp.int32)
        end = jnp.int32(0)
        for doc in range(len_ref.shape[1]):
            end = end + len_ref[stream, doc]
            first = jnp.maximum(first, jnp.where(row + base >= end, end, 0))
        for r in range(n_cp + 1):
            allowed = lane + (base - r * rows) >= first
            if r == 0:
                allowed = allowed & (lane <= row)
            bias[:, r * rows : (r + 1) * rows] = jnp.where(allowed, 0.0, NEGATIVE)

        mask = jnp.concatenate([bias[...]] * group, axis=0)
        query_copy(ch).wait()
        for head in range(heads):
            k_cols = slice(head * HEAD_WIDTH, (head + 1) * HEAD_WIDTH)
            v_cols = slice(part + head * HEAD_WIDTH, part + (head + 1) * HEAD_WIDTH)
            k_all = jnp.concatenate([kv[r, ch, :, k_cols] for r in range(n_cp + 1)], axis=0)
            v_all = jnp.concatenate([kv[r, ch, :, v_cols] for r in range(n_cp + 1)], axis=0)

            def q_cols(j):
                at = ((piece * heads + head) * group + j) * HEAD_WIDTH
                return pl.ds(pl.multiple_of(at, HEAD_WIDTH), HEAD_WIDTH)

            scores = lax.dot_general(
                jnp.concatenate([q_buf[stream, :, q_cols(j)] for j in range(group)], axis=0),
                k_all,
                (((1,), (1,)), ((), ())),
                preferred_element_type=jnp.float32,
            )
            scores = scores + mask
            largest = jnp.max(scores, axis=1, keepdims=True)
            probs = jnp.exp2((scores - largest) * (HEAD_WIDTH**-0.5 * LOG2_E))
            total = jnp.sum(probs, axis=1, keepdims=True)
            summed = jnp.dot(probs.astype(jnp.bfloat16), v_all, preferred_element_type=jnp.float32)
            result = (summed / total).astype(o_buf.dtype)
            for j in range(group):
                o_buf[stream, :, q_cols(j)] = result[j * rows : (j + 1) * rows]
        result_copy(ch).start()

    @pl.loop(0, chunks + nz)
    def _(t):
        @pl.when(t < chunks)
        def _():
            local(t, 0).wait()
            local(t, 1).wait()
            remote(0, 2 * nz, t, hop_row, next_line).start()

            @pl.when(z < nz - 1)
            def _():
                remote(0, 2, t, fwd_row, up).start()

            to_partner(0, t)

        for d in range(nz, 0, -1):
            ch = t - (nz + 1 - d)

            @pl.when((ch >= 0) & (ch < chunks) & (z < d))
            def _():
                arrived(2 * d, ch)
                if d > 1:

                    @pl.when(z > 0)
                    def _():
                        remote(2 * d, 2 * d - 2, ch, bwd_row + d, down).start()

                to_partner(d, ch)

        for d in range(1, nz):
            ch = t - d

            @pl.when((ch >= 0) & (ch < chunks) & (z >= d))
            def _():
                arrived(2 * d, ch)
                if d < nz - 1:

                    @pl.when(z < nz - 1)
                    def _():
                        remote(2 * d, 2 * d + 2, ch, fwd_row + d, up).start()

                to_partner(d, ch)

        @pl.when(t >= nz)
        def _():
            ch = t - nz
            for d in range(nz):
                arrived(2 * d + 1, ch)
            attend(ch)

    @pl.loop(0, chunks)
    def _(ch):
        def sent(row):
            remote(0, 1, ch, row, partner).wait_send()

        result_copy(ch).wait()
        sent(hop_row)
        for d in range(nz - 1):

            @pl.when((z >= d) & (z < nz - 1))
            def _():
                sent(fwd_row + d)

        for d in range(2, nz + 1):

            @pl.when((z < d) & (z > 0))
            def _():
                sent(bwd_row + d)

        for d in range(nz + 1):
            if d == 0:

                @pl.when(core == 0)
                def _():
                    sent(mate_row)

            elif d == nz:

                @pl.when(core == 1)
                def _():
                    sent(mate_row + nz)

            else:
                sent(mate_row + d)


def by_window(n_grp, n_cp, queries, keys, values, doc_lengths):
    streams, rows, _ = queries.shape
    chunks = streams * PARTS
    width = 2 * keys.shape[2] // PARTS
    window = (n_cp + 1) * rows
    nz = n_cp // 2
    pairs = streams * QUERY_HEADS * rows * window
    return pl.pallas_call(
        functools.partial(window_kernel, n_grp, n_cp, streams),
        out_shape=jax.ShapeDtypeStruct(queries.shape, queries.dtype),
        in_specs=[
            pl.BlockSpec(memory_space=pl.ANY),
            pl.BlockSpec(memory_space=pl.ANY),
            pl.BlockSpec(memory_space=pl.ANY),
            pl.BlockSpec(memory_space=pltpu.SMEM),
        ],
        out_specs=pl.BlockSpec(memory_space=pl.ANY),
        scratch_shapes=[
            pltpu.VMEM((n_cp + 1, chunks, rows, width), keys.dtype),
            pltpu.VMEM(queries.shape, queries.dtype),
            pltpu.VMEM(queries.shape, queries.dtype),
            pltpu.VMEM((rows, window), jnp.float32),
            pltpu.SemaphoreType.DMA((4, chunks)),
            pltpu.SemaphoreType.DMA((3 * nz, chunks)),
            pltpu.SemaphoreType.DMA((n_cp + 1, chunks)),
        ],
        cost_estimate=pl.CostEstimate(
            flops=4 * pairs * HEAD_WIDTH, bytes_accessed=5 * queries.size, transcendentals=pairs
        ),
        compiler_params=pltpu.CompilerParams(
            collective_id=0, has_side_effects=True, vmem_limit_bytes=56 * 2**20
        ),
        name="window_attention",
    )(queries, keys, values, doc_lengths)


def window_fits(n_grp, n_cp, queries, keys):
    line = 2 * keys.shape[0] * keys.shape[1] // n_grp * keys.shape[2] * keys.dtype.itemsize
    return n_cp % 2 == 0 and n_cp >= 4 and n_grp >= 3 and line <= WINDOW_BYTES


def doc_of(positions, ends):
    return jnp.sum((positions[:, None] >= ends[None, :]).astype(jnp.int32), axis=1)


def doc_first(positions, ends):
    return jnp.max(jnp.where(ends[None, :] <= positions[:, None], ends[None, :], 0), axis=1)


def absorb(state, scores, allowed, value_portion):
    running_max, running_sum, running_acc = state
    scores = jnp.where(allowed, scores, NEGATIVE)
    new_max = jnp.maximum(running_max, jnp.max(scores, axis=-1))
    factor = jnp.exp(running_max - new_max)
    probs = jnp.where(allowed, jnp.exp(scores - new_max[..., None]), 0.0)
    new_sum = running_sum * factor + jnp.sum(probs, axis=-1)
    product = jnp.einsum(
        "hqk,khd->hqd",
        probs.astype(jnp.bfloat16),
        value_portion,
        preferred_element_type=jnp.float32,
    )
    return (new_max, new_sum, running_acc * factor[..., None] + product)


def attend_stream(query_seq, key_seq, value_seq, ends):
    stream_len = query_seq.shape[0]
    items = query_seq.shape[1]
    scale = HEAD_WIDTH ** (-0.5)
    positions = jnp.arange(stream_len, dtype=jnp.int32)
    all_docs = doc_of(positions, ends)
    all_firsts = doc_first(positions, ends)
    span = min(512, stream_len)
    spans = stream_len // span

    def query_span(number):
        begin = number * span
        query_tile = lax.dynamic_slice_in_dim(query_seq, begin, span, 0)
        query_pos = lax.dynamic_slice_in_dim(positions, begin, span, 0)
        query_doc = lax.dynamic_slice_in_dim(all_docs, begin, span, 0)
        first_span = lax.dynamic_index_in_dim(all_firsts, begin, 0, keepdims=False) // span

        def key_span(other, state):
            offset = other * span
            key_tile = lax.dynamic_slice_in_dim(key_seq, offset, span, 0)
            value_tile = lax.dynamic_slice_in_dim(value_seq, offset, span, 0)
            key_pos = lax.dynamic_slice_in_dim(positions, offset, span, 0)
            key_doc = lax.dynamic_slice_in_dim(all_docs, offset, span, 0)
            allowed = (key_pos[None, :] <= query_pos[:, None]) & (
                key_doc[None, :] == query_doc[:, None]
            )
            scores = (
                jnp.einsum("qhd,khd->hqk", query_tile, key_tile, preferred_element_type=jnp.float32)
                * scale
            )
            return absorb(state, scores, allowed, value_tile)

        start_state = (
            jnp.full((items, span), NEGATIVE, jnp.float32),
            jnp.zeros((items, span), jnp.float32),
            jnp.zeros((items, span, HEAD_WIDTH), jnp.float32),
        )
        final_max, final_sum, final_acc = lax.fori_loop(
            first_span, number + 1, key_span, start_state
        )
        return (final_acc / final_sum[..., None]).transpose(1, 0, 2).astype(jnp.bfloat16)

    tiles = lax.map(query_span, jnp.arange(spans, dtype=jnp.int32))
    return tiles.reshape(stream_len, items, HEAD_WIDTH)


def on_device(queries, keys, values, doc_lengths):
    n_ranks = lax.axis_size("cp")
    n_streams = queries.shape[0]
    rows_per = queries.shape[1]
    group_count = QUERY_HEADS // KEY_VALUE_HEADS
    per_rank = QUERY_HEADS // n_ranks
    stream_id = lax.axis_index("grp")
    lengths_row = lax.dynamic_index_in_dim(doc_lengths, stream_id, 0, keepdims=False)
    ends = jnp.cumsum(lengths_row)

    def by_heads(array):
        shaped = array.reshape(n_streams, rows_per, n_ranks, per_rank, HEAD_WIDTH)
        return shaped.transpose(0, 2, 1, 3, 4).reshape(
            n_streams * n_ranks, rows_per, per_rank, HEAD_WIDTH
        )

    key_wide = jnp.repeat(
        keys.reshape(n_streams, rows_per, KEY_VALUE_HEADS, HEAD_WIDTH), group_count, axis=2
    )
    value_wide = jnp.repeat(
        values.reshape(n_streams, rows_per, KEY_VALUE_HEADS, HEAD_WIDTH), group_count, axis=2
    )
    query_split = by_heads(queries)
    key_divided_rows = by_heads(key_wide)
    value_divided_rows = by_heads(value_wide)
    query_part = lax.all_to_all(query_split, ("grp", "cp"), split_axis=0, concat_axis=1, tiled=True)
    key_portion = lax.all_to_all(
        key_divided_rows, ("grp", "cp"), split_axis=0, concat_axis=1, tiled=True
    )
    value_portion = lax.all_to_all(
        value_divided_rows, ("grp", "cp"), split_axis=0, concat_axis=1, tiled=True
    )
    outcome = attend_stream(query_part[0], key_portion[0], value_portion[0], ends)
    head_output = outcome[None]
    returned = lax.all_to_all(head_output, ("grp", "cp"), split_axis=1, concat_axis=0, tiled=True)
    shaped = returned.reshape(n_streams, n_ranks, rows_per, per_rank, HEAD_WIDTH).transpose(
        0, 2, 1, 3, 4
    )
    return shaped.reshape(n_streams, rows_per, QUERY_HEADS * HEAD_WIDTH)


def solution(mesh):
    n_grp, n_cp = mesh.shape["grp"], mesh.shape["cp"]
    placed = (
        P(None, ("grp", "cp"), None),
        P(None, ("grp", "cp"), None),
        P(None, ("grp", "cp"), None),
        P(),
    )

    def run(queries, keys, values, doc_lengths):
        if window_fits(n_grp, n_cp, queries, keys):
            plan = functools.partial(by_window, n_grp, n_cp)
        else:
            plan = on_device
        return jax.shard_map(
            plan,
            mesh=mesh,
            in_specs=placed,
            out_specs=P(None, ("grp", "cp"), None),
            check_vma=False,
        )(queries, keys, values, doc_lengths)

    return run
```

```python
import functools

import jax
import jax.numpy as jnp
from jax import lax
from jax.experimental import pallas as pl
from jax.experimental.pallas import tpu as pltpu
from jax.sharding import PartitionSpec as P

MESH = pl.DeviceIdType.MESH
PARTS = 4
MOVED = 4
OFF = 2
WINDOW_BYTES = 40 * 2**20

QUERY_HEADS = 32
KEY_VALUE_HEADS = 8
HEAD_WIDTH = 128
NEGATIVE = -1e30
LOG2_E = 1.4426950408889634


def window_kernel(
    n_grp,
    n_cp,
    streams,
    q_ref,
    k_ref,
    v_ref,
    len_ref,
    o_ref,
    kv,
    q_buf,
    o_buf,
    bias,
    local_sem,
    send_sem,
    recv_sem,
):
    grp, cp = lax.axis_index("grp"), lax.axis_index("cp")
    z, core = cp // 2, cp % 2
    nz = n_cp // 2
    last = nz - 1
    chunks = streams * PARTS
    rows = k_ref.shape[1]
    part = k_ref.shape[2] // PARTS
    heads = part // HEAD_WIDTH
    group = QUERY_HEADS // KEY_VALUE_HEADS
    wide = part * group
    partner = (grp, z * 2 + 1 - core)
    up = (grp, cp + 2)
    down = (grp, cp - 2)
    next_line = ((grp + 1) % n_grp, cp)
    prev_line = ((grp + n_grp - 1) % n_grp, cp)
    fwd_row, hop_row, bwd_row, mate_row = 0, nz - 1, nz - 2, 2 * nz - 1
    far_row, ahead_row, edge_row, ask_row, answer_row = (3 * nz + i for i in range(5))
    ask_slot, answer_slot = n_cp + 2 * OFF + 1, n_cp + 2 * OFF + 2
    at_end = (z == 0) | (z == last)
    helper = (z == 1) | (z == last - 1)

    def moved(ch):
        return ch % MOVED == 0

    def normal(ch):
        return jnp.logical_not(moved(ch) & at_end)

    def local(ch, which):
        source = (k_ref, v_ref)[which]
        cols = pl.ds(pl.multiple_of((ch % PARTS) * part, part), part)
        return pltpu.make_async_copy(
            source.at[ch // PARTS, :, cols],
            kv.at[OFF, ch, :, pl.ds(which * part, part)],
            local_sem.at[which, ch],
        )

    def own_columns(ch):
        return ch // PARTS, slice(None), pl.ds(pl.multiple_of((ch % PARTS) * wide, wide), wide)

    def query_copy(ch):
        return pltpu.make_async_copy(q_ref.at[own_columns(ch)], q_buf.at[ch], local_sem.at[2, ch])

    def result_copy(ch):
        return pltpu.make_async_copy(o_buf.at[ch], o_ref.at[own_columns(ch)], local_sem.at[3, ch])

    def remote(source, target, ch, row, device):
        return pltpu.make_async_remote_copy(
            src_ref=kv.at[OFF + source, ch],
            dst_ref=kv.at[OFF + target, ch],
            send_sem=send_sem.at[row, ch],
            recv_sem=recv_sem.at[OFF + target, ch],
            device_id=device,
            device_id_type=MESH,
        )

    def arrived(slot, ch):
        remote(slot, slot, ch, 0, partner).wait_recv()

    def ask(ch, device):
        return pltpu.make_async_remote_copy(
            src_ref=q_buf.at[ch],
            dst_ref=q_buf.at[chunks + ch // MOVED],
            send_sem=send_sem.at[ask_row, ch],
            recv_sem=recv_sem.at[ask_slot, ch],
            device_id=device,
            device_id_type=MESH,
        )

    def answer(ch, device):
        return pltpu.make_async_remote_copy(
            src_ref=o_buf.at[chunks + ch // MOVED],
            dst_ref=o_buf.at[ch],
            send_sem=send_sem.at[answer_row, ch],
            recv_sem=recv_sem.at[answer_slot, ch],
            device_id=device,
            device_id_type=MESH,
        )

    @pl.loop(0, chunks)
    def _(ch):
        local(ch, 0).start()
        local(ch, 1).start()

    @pl.loop(0, chunks)
    def _(ch):
        query_copy(ch).start()

    barrier = pltpu.get_barrier_semaphore()

    def greet(device):
        pl.semaphore_signal(barrier, inc=1, device_id=device, device_id_type=MESH)

    greet(partner)
    greet(next_line)
    greet(prev_line)

    @pl.when(z < last)
    def _():
        greet(up)

    @pl.when(z > 0)
    def _():
        greet(down)

    pl.semaphore_wait(barrier, jnp.where(at_end, 4, 5))

    def to_partner(d, ch):
        if d < nz:

            @pl.when(core == 0)
            def _():
                remote(2 * d, 2 * d + 1, ch, mate_row + d, partner).start()

        if d > 0:

            @pl.when(core == 1)
            def _():
                remote(2 * d, 2 * d - 1, ch, mate_row + d, partner).start()

    def attend(ch, q_at, shift):
        stream = ch // PARTS
        base = (grp * n_cp + cp - shift) * rows
        row = lax.broadcasted_iota(jnp.int32, (rows, rows), 0)
        lane = lax.broadcasted_iota(jnp.int32, (rows, rows), 1)
        first = jnp.zeros((rows, rows), jnp.int32)
        end = jnp.int32(0)
        for doc in range(len_ref.shape[1]):
            end = end + len_ref[stream, doc]
            first = jnp.maximum(first, jnp.where(row + base >= end, end, 0))
        for r in range(n_cp + 1):
            allowed = lane + (base - r * rows) >= first
            if r == 0:
                allowed = allowed & (lane <= row)
            bias[:, r * rows : (r + 1) * rows] = jnp.where(allowed, 0.0, NEGATIVE)

        mask = jnp.concatenate([bias[...]] * group, axis=0)
        slots = [OFF + shift + r for r in range(n_cp + 1)]
        for head in range(heads):
            k_cols = slice(head * HEAD_WIDTH, (head + 1) * HEAD_WIDTH)
            v_cols = slice(part + head * HEAD_WIDTH, part + (head + 1) * HEAD_WIDTH)
            k_all = jnp.concatenate([kv[slot, ch, :, k_cols] for slot in slots], axis=0)
            v_all = jnp.concatenate([kv[slot, ch, :, v_cols] for slot in slots], axis=0)

            def q_cols(j):
                at = (head * group + j) * HEAD_WIDTH
                return slice(at, at + HEAD_WIDTH)

            scores = lax.dot_general(
                jnp.concatenate([q_buf[q_at, :, q_cols(j)] for j in range(group)], axis=0),
                k_all,
                (((1,), (1,)), ((), ())),
                preferred_element_type=jnp.float32,
            )
            scores = scores + mask
            largest = jnp.max(scores, axis=1, keepdims=True)
            probs = jnp.exp2((scores - largest) * (HEAD_WIDTH**-0.5 * LOG2_E))
            total = jnp.sum(probs, axis=1, keepdims=True)
            summed = jnp.dot(probs.astype(jnp.bfloat16), v_all, preferred_element_type=jnp.float32)
            result = (summed / total).astype(o_buf.dtype)
            for j in range(group):
                o_buf[q_at, :, q_cols(j)] = result[j * rows : (j + 1) * rows]

    @pl.loop(0, chunks + nz)
    def _(t):
        @pl.when(t < chunks)
        def _():
            local(t, 0).wait()
            local(t, 1).wait()

            @pl.when(normal(t))
            def _():
                remote(0, 2 * nz, t, hop_row, next_line).start()

            @pl.when((z < last) & (jnp.logical_not(moved(t)) | (z < last - 1)))
            def _():
                remote(0, 2, t, fwd_row, up).start()

            @pl.when(moved(t) & (z == last))
            def _():
                remote(0, -2, t, ahead_row, down).start()

            @pl.when(normal(t))
            def _():
                to_partner(0, t)

            @pl.when(moved(t) & (z == last - 1) & (core == 1))
            def _():
                remote(0, -1, t, edge_row, partner).start()

        for d in range(nz, 0, -1):
            ch = t - (nz + 1 - d)

            @pl.when((ch >= 0) & (ch < chunks) & (z < d) & normal(ch))
            def _():
                arrived(2 * d, ch)
                if d > 1:

                    @pl.when((z > 0) & (jnp.logical_not(moved(ch)) | (z > 1)))
                    def _():
                        remote(2 * d, 2 * d - 2, ch, bwd_row + d, down).start()

                to_partner(d, ch)
                if d == nz:

                    @pl.when(moved(ch) & (z == 1) & (core == 0))
                    def _():
                        remote(2 * nz, 2 * nz + 1, ch, edge_row, partner).start()

        for d in range(1, nz):
            ch = t - d

            @pl.when((ch >= 0) & (ch < chunks) & (z >= d) & normal(ch))
            def _():
                arrived(2 * d, ch)
                if d < nz - 1:

                    @pl.when((z < last) & (jnp.logical_not(moved(ch)) | (z < last - 1)))
                    def _():
                        remote(2 * d, 2 * d + 2, ch, fwd_row + d, up).start()

                to_partner(d, ch)
                if d == 1:

                    @pl.when(moved(ch) & (z == 1))
                    def _():
                        remote(2, 2 * nz + 2, ch, far_row, next_line).start()

        before = t - 1

        @pl.when((before >= 0) & (before < chunks) & moved(before))
        def _():
            @pl.when(at_end)
            def _():
                query_copy(before).wait()

            @pl.when(z == 0)
            def _():
                ask(before, up).start()

            @pl.when(z == last)
            def _():
                ask(before, down).start()

            @pl.when(z == last - 1)
            def _():
                arrived(-2, before)
                remote(-2, 2 * nz - 2, before, far_row, next_line).start()

                @pl.when(core == 0)
                def _():
                    remote(-2, -1, before, edge_row, partner).start()

        earlier = t - 2

        @pl.when((earlier >= 0) & (earlier < chunks) & moved(earlier) & (z == 1))
        def _():
            arrived(2 * nz + 2, earlier)

            @pl.when(core == 1)
            def _():
                remote(2 * nz + 2, 2 * nz + 1, earlier, edge_row, partner).start()

        ch = t - nz

        @pl.when((ch >= 0) & normal(ch))
        def _():
            for d in range(nz):
                arrived(2 * d + 1, ch)
            query_copy(ch).wait()
            helps = helper & moved(ch)

            @pl.when(helps)
            def _():
                ask(ch, partner).wait_recv()

                @pl.when(z == 1)
                def _():
                    arrived(2 * nz + 1, ch)

                @pl.when(z == last - 1)
                def _():
                    arrived(-1, ch)

            @pl.loop(jnp.where(helps, 0, 1), 2)
            def _(own):
                other = 1 - own
                attend(
                    ch,
                    other * (chunks + ch // MOVED) + own * ch,
                    other * jnp.where(z == 1, 2, -2),
                )

                @pl.when(other == 1)
                def _():
                    @pl.when(z == 1)
                    def _():
                        answer(ch, down).start()

                    @pl.when(z == last - 1)
                    def _():
                        answer(ch, up).start()

            result_copy(ch).start()

    @pl.loop(0, chunks)
    def _(ch):
        def sent(row):
            remote(0, 1, ch, row, partner).wait_send()

        @pl.when(moved(ch) & at_end)
        def _():
            answer(ch, partner).wait_recv()
            result_copy(ch).start()
            ask(ch, partner).wait_send()

        result_copy(ch).wait()

        @pl.when(moved(ch) & helper)
        def _():
            sent(far_row)
            sent(edge_row)
            answer(ch, partner).wait_send()

        @pl.when(moved(ch) & (z == last))
        def _():
            sent(ahead_row)

        for d in range(nz - 1):

            @pl.when((z >= d) & (z < last) & (jnp.logical_not(moved(ch)) | (z < last - 1)))
            def _():
                sent(fwd_row + d)

        for d in range(2, nz + 1):

            @pl.when((z < d) & (z > 0) & (jnp.logical_not(moved(ch)) | ((z > 1) & (z < last))))
            def _():
                sent(bwd_row + d)

        @pl.when(normal(ch))
        def _():
            sent(hop_row)
            for d in range(nz + 1):
                if d == 0:

                    @pl.when(core == 0)
                    def _():
                        sent(mate_row)

                elif d == nz:

                    @pl.when(core == 1)
                    def _():
                        sent(mate_row + nz)

                else:
                    sent(mate_row + d)


def by_window(n_grp, n_cp, queries, keys, values, doc_lengths):
    streams, rows, _ = queries.shape
    chunks = streams * PARTS
    width = 2 * keys.shape[2] // PARTS
    window = (n_cp + 1) * rows
    nz = n_cp // 2
    pairs = streams * QUERY_HEADS * rows * window
    held = (chunks + chunks // MOVED, rows, queries.shape[2] // PARTS)
    return pl.pallas_call(
        functools.partial(window_kernel, n_grp, n_cp, streams),
        out_shape=jax.ShapeDtypeStruct(queries.shape, queries.dtype),
        in_specs=[
            pl.BlockSpec(memory_space=pl.ANY),
            pl.BlockSpec(memory_space=pl.ANY),
            pl.BlockSpec(memory_space=pl.ANY),
            pl.BlockSpec(memory_space=pltpu.SMEM),
        ],
        out_specs=pl.BlockSpec(memory_space=pl.ANY),
        scratch_shapes=[
            pltpu.VMEM((n_cp + 1 + 2 * OFF, chunks, rows, width), keys.dtype),
            pltpu.VMEM(held, queries.dtype),
            pltpu.VMEM(held, queries.dtype),
            pltpu.VMEM((rows, window), jnp.float32),
            pltpu.SemaphoreType.DMA((4, chunks)),
            pltpu.SemaphoreType.DMA((3 * nz + 5, chunks)),
            pltpu.SemaphoreType.DMA((n_cp + 3 + 2 * OFF, chunks)),
        ],
        cost_estimate=pl.CostEstimate(
            flops=4 * pairs * HEAD_WIDTH, bytes_accessed=5 * queries.size, transcendentals=pairs
        ),
        compiler_params=pltpu.CompilerParams(
            collective_id=0, has_side_effects=True, vmem_limit_bytes=56 * 2**20
        ),
        name="window_attention",
    )(queries, keys, values, doc_lengths)


def window_fits(n_grp, n_cp, queries, keys):
    line = 2 * keys.shape[0] * keys.shape[1] // n_grp * keys.shape[2] * keys.dtype.itemsize
    return n_cp % 2 == 0 and n_cp >= 8 and n_grp >= 3 and line <= WINDOW_BYTES


def doc_of(positions, ends):
    return jnp.sum((positions[:, None] >= ends[None, :]).astype(jnp.int32), axis=1)


def doc_first(positions, ends):
    return jnp.max(jnp.where(ends[None, :] <= positions[:, None], ends[None, :], 0), axis=1)


def absorb(state, scores, allowed, value_portion):
    running_max, running_sum, running_acc = state
    scores = jnp.where(allowed, scores, NEGATIVE)
    new_max = jnp.maximum(running_max, jnp.max(scores, axis=-1))
    factor = jnp.exp(running_max - new_max)
    probs = jnp.where(allowed, jnp.exp(scores - new_max[..., None]), 0.0)
    new_sum = running_sum * factor + jnp.sum(probs, axis=-1)
    product = jnp.einsum(
        "hqk,khd->hqd",
        probs.astype(jnp.bfloat16),
        value_portion,
        preferred_element_type=jnp.float32,
    )
    return (new_max, new_sum, running_acc * factor[..., None] + product)


def attend_stream(query_seq, key_seq, value_seq, ends):
    stream_len = query_seq.shape[0]
    items = query_seq.shape[1]
    scale = HEAD_WIDTH ** (-0.5)
    positions = jnp.arange(stream_len, dtype=jnp.int32)
    all_docs = doc_of(positions, ends)
    all_firsts = doc_first(positions, ends)
    span = min(512, stream_len)
    spans = stream_len // span

    def query_span(number):
        begin = number * span
        query_tile = lax.dynamic_slice_in_dim(query_seq, begin, span, 0)
        query_pos = lax.dynamic_slice_in_dim(positions, begin, span, 0)
        query_doc = lax.dynamic_slice_in_dim(all_docs, begin, span, 0)
        first_span = lax.dynamic_index_in_dim(all_firsts, begin, 0, keepdims=False) // span

        def key_span(other, state):
            offset = other * span
            key_tile = lax.dynamic_slice_in_dim(key_seq, offset, span, 0)
            value_tile = lax.dynamic_slice_in_dim(value_seq, offset, span, 0)
            key_pos = lax.dynamic_slice_in_dim(positions, offset, span, 0)
            key_doc = lax.dynamic_slice_in_dim(all_docs, offset, span, 0)
            allowed = (key_pos[None, :] <= query_pos[:, None]) & (
                key_doc[None, :] == query_doc[:, None]
            )
            scores = (
                jnp.einsum("qhd,khd->hqk", query_tile, key_tile, preferred_element_type=jnp.float32)
                * scale
            )
            return absorb(state, scores, allowed, value_tile)

        start_state = (
            jnp.full((items, span), NEGATIVE, jnp.float32),
            jnp.zeros((items, span), jnp.float32),
            jnp.zeros((items, span, HEAD_WIDTH), jnp.float32),
        )
        final_max, final_sum, final_acc = lax.fori_loop(
            first_span, number + 1, key_span, start_state
        )
        return (final_acc / final_sum[..., None]).transpose(1, 0, 2).astype(jnp.bfloat16)

    tiles = lax.map(query_span, jnp.arange(spans, dtype=jnp.int32))
    return tiles.reshape(stream_len, items, HEAD_WIDTH)


def on_device(queries, keys, values, doc_lengths):
    n_ranks = lax.axis_size("cp")
    n_streams = queries.shape[0]
    rows_per = queries.shape[1]
    group_count = QUERY_HEADS // KEY_VALUE_HEADS
    per_rank = QUERY_HEADS // n_ranks
    stream_id = lax.axis_index("grp")
    lengths_row = lax.dynamic_index_in_dim(doc_lengths, stream_id, 0, keepdims=False)
    ends = jnp.cumsum(lengths_row)

    def by_heads(array):
        shaped = array.reshape(n_streams, rows_per, n_ranks, per_rank, HEAD_WIDTH)
        return shaped.transpose(0, 2, 1, 3, 4).reshape(
            n_streams * n_ranks, rows_per, per_rank, HEAD_WIDTH
        )

    key_wide = jnp.repeat(
        keys.reshape(n_streams, rows_per, KEY_VALUE_HEADS, HEAD_WIDTH), group_count, axis=2
    )
    value_wide = jnp.repeat(
        values.reshape(n_streams, rows_per, KEY_VALUE_HEADS, HEAD_WIDTH), group_count, axis=2
    )
    query_split = by_heads(queries)
    key_divided_rows = by_heads(key_wide)
    value_divided_rows = by_heads(value_wide)
    query_part = lax.all_to_all(query_split, ("grp", "cp"), split_axis=0, concat_axis=1, tiled=True)
    key_portion = lax.all_to_all(
        key_divided_rows, ("grp", "cp"), split_axis=0, concat_axis=1, tiled=True
    )
    value_portion = lax.all_to_all(
        value_divided_rows, ("grp", "cp"), split_axis=0, concat_axis=1, tiled=True
    )
    outcome = attend_stream(query_part[0], key_portion[0], value_portion[0], ends)
    head_output = outcome[None]
    returned = lax.all_to_all(head_output, ("grp", "cp"), split_axis=1, concat_axis=0, tiled=True)
    shaped = returned.reshape(n_streams, n_ranks, rows_per, per_rank, HEAD_WIDTH).transpose(
        0, 2, 1, 3, 4
    )
    return shaped.reshape(n_streams, rows_per, QUERY_HEADS * HEAD_WIDTH)


def solution(mesh):
    n_grp, n_cp = mesh.shape["grp"], mesh.shape["cp"]
    placed = (
        P(None, ("grp", "cp"), None),
        P(None, ("grp", "cp"), None),
        P(None, ("grp", "cp"), None),
        P(),
    )

    def run(queries, keys, values, doc_lengths):
        if window_fits(n_grp, n_cp, queries, keys):
            plan = functools.partial(by_window, n_grp, n_cp)
        else:
            plan = on_device
        return jax.shard_map(
            plan,
            mesh=mesh,
            in_specs=placed,
            out_specs=P(None, ("grp", "cp"), None),
            check_vma=False,
        )(queries, keys, values, doc_lengths)

    return run
```

```python
import functools

import jax
import jax.numpy as jnp
from jax import lax
from jax.experimental import pallas as pl
from jax.experimental.pallas import tpu as pltpu
from jax.sharding import PartitionSpec as P

MESH = pl.DeviceIdType.MESH
PARTS = 4
MOVED = 2
BLOCK = 32
OFF = 2
WINDOW_BYTES = 40 * 2**20

QUERY_HEADS = 32
KEY_VALUE_HEADS = 8
HEAD_WIDTH = 128
NEGATIVE = -1e30
LOG2_E = 1.4426950408889634


def window_kernel(
    n_grp,
    n_cp,
    streams,
    q_ref,
    k_ref,
    v_ref,
    len_ref,
    o_ref,
    kv,
    q_buf,
    o_buf,
    bias,
    scores_buf,
    weights_buf,
    inverse_buf,
    local_sem,
    send_sem,
    recv_sem,
):
    grp, cp = lax.axis_index("grp"), lax.axis_index("cp")
    z, core = cp // 2, cp % 2
    nz = n_cp // 2
    last = nz - 1
    chunks = streams * PARTS
    rows = k_ref.shape[1]
    part = k_ref.shape[2] // PARTS
    heads = part // HEAD_WIDTH
    group = QUERY_HEADS // KEY_VALUE_HEADS
    wide = part * group
    partner = (grp, z * 2 + 1 - core)
    up = (grp, cp + 2)
    down = (grp, cp - 2)
    next_line = ((grp + 1) % n_grp, cp)
    prev_line = ((grp + n_grp - 1) % n_grp, cp)
    fwd_row, hop_row, bwd_row, mate_row = 0, nz - 1, nz - 2, 2 * nz - 1
    far_row, ahead_row, edge_row, ask_row, answer_row = (3 * nz + i for i in range(5))
    ask_slot, answer_slot = n_cp + 2 * OFF + 1, n_cp + 2 * OFF + 2
    at_end = (z == 0) | (z == last)
    helper = (z == 1) | (z == last - 1)

    def moved(ch):
        return ch % MOVED == 0

    def normal(ch):
        return jnp.logical_not(moved(ch) & at_end)

    def local(ch, which):
        source = (k_ref, v_ref)[which]
        cols = pl.ds(pl.multiple_of((ch % PARTS) * part, part), part)
        return pltpu.make_async_copy(
            source.at[ch // PARTS, :, cols],
            kv.at[OFF, ch, :, pl.ds(which * part, part)],
            local_sem.at[which, ch],
        )

    def own_columns(ch):
        return ch // PARTS, slice(None), pl.ds(pl.multiple_of((ch % PARTS) * wide, wide), wide)

    def query_copy(ch):
        return pltpu.make_async_copy(q_ref.at[own_columns(ch)], q_buf.at[ch], local_sem.at[2, ch])

    def result_copy(ch):
        return pltpu.make_async_copy(o_buf.at[ch], o_ref.at[own_columns(ch)], local_sem.at[3, ch])

    def remote(source, target, ch, row, device):
        return pltpu.make_async_remote_copy(
            src_ref=kv.at[OFF + source, ch],
            dst_ref=kv.at[OFF + target, ch],
            send_sem=send_sem.at[row, ch],
            recv_sem=recv_sem.at[OFF + target, ch],
            device_id=device,
            device_id_type=MESH,
        )

    def arrived(slot, ch):
        remote(slot, slot, ch, 0, partner).wait_recv()

    def ask(ch, device):
        return pltpu.make_async_remote_copy(
            src_ref=q_buf.at[ch],
            dst_ref=q_buf.at[chunks + ch // MOVED],
            send_sem=send_sem.at[ask_row, ch],
            recv_sem=recv_sem.at[ask_slot, ch],
            device_id=device,
            device_id_type=MESH,
        )

    def answer(ch, device):
        return pltpu.make_async_remote_copy(
            src_ref=o_buf.at[chunks + ch // MOVED],
            dst_ref=o_buf.at[ch],
            send_sem=send_sem.at[answer_row, ch],
            recv_sem=recv_sem.at[answer_slot, ch],
            device_id=device,
            device_id_type=MESH,
        )

    @pl.loop(0, chunks)
    def _(ch):
        local(ch, 0).start()
        local(ch, 1).start()

    @pl.loop(0, chunks)
    def _(ch):
        query_copy(ch).start()

    barrier = pltpu.get_barrier_semaphore()

    def greet(device):
        pl.semaphore_signal(barrier, inc=1, device_id=device, device_id_type=MESH)

    greet(partner)
    greet(next_line)
    greet(prev_line)

    @pl.when(z < last)
    def _():
        greet(up)

    @pl.when(z > 0)
    def _():
        greet(down)

    pl.semaphore_wait(barrier, jnp.where(at_end, 4, 5))

    def to_partner(d, ch):
        if d < nz:

            @pl.when(core == 0)
            def _():
                remote(2 * d, 2 * d + 1, ch, mate_row + d, partner).start()

        if d > 0:

            @pl.when(core == 1)
            def _():
                remote(2 * d, 2 * d - 1, ch, mate_row + d, partner).start()

    def attend(ch, q_at, shift):
        stream = ch // PARTS
        base = (grp * n_cp + cp - shift) * rows
        row = lax.broadcasted_iota(jnp.int32, (rows, rows), 0)
        lane = lax.broadcasted_iota(jnp.int32, (rows, rows), 1)
        first = jnp.zeros((rows, rows), jnp.int32)
        end = jnp.int32(0)
        for doc in range(len_ref.shape[1]):
            end = end + len_ref[stream, doc]
            first = jnp.maximum(first, jnp.where(row + base >= end, end, 0))
        for r in range(n_cp + 1):
            allowed = lane + (base - r * rows) >= first
            if r == 0:
                allowed = allowed & (lane <= row)
            bias[:, r * rows : (r + 1) * rows] = jnp.where(allowed, 0.0, NEGATIVE)

        slots = [OFF + shift + r for r in range(n_cp + 1)]

        def q_cols(head, j):
            at = (head * group + j) * HEAD_WIDTH
            return slice(at, at + HEAD_WIDTH)

        for head in range(heads):
            k_cols = slice(head * HEAD_WIDTH, (head + 1) * HEAD_WIDTH)
            scores_buf[head] = lax.dot_general(
                jnp.concatenate([q_buf[q_at, :, q_cols(head, j)] for j in range(group)], axis=0),
                jnp.concatenate([kv[slot, ch, :, k_cols] for slot in slots], axis=0),
                (((1,), (1,)), ((), ())),
                preferred_element_type=jnp.float32,
            )

        def normalise(i, carry):
            at = pl.ds(pl.multiple_of(i * BLOCK, BLOCK), BLOCK)
            token = pl.ds(pl.multiple_of(i % (rows // BLOCK) * BLOCK, BLOCK), BLOCK)
            mask = bias[token, :]
            for head in range(heads):
                scores = scores_buf[head, at, :] + mask
                largest = jnp.max(scores, axis=1, keepdims=True)
                probs = jnp.exp2((scores - largest) * (HEAD_WIDTH**-0.5 * LOG2_E))
                total = jnp.sum(probs, axis=1, keepdims=True)
                weights_buf[head, at, :] = probs.astype(jnp.bfloat16)
                inverse_buf[head, at, :] = jnp.broadcast_to(1.0 / total, (BLOCK, HEAD_WIDTH))
            return carry

        lax.fori_loop(0, group * rows // BLOCK, normalise, 0, unroll=2)

        for head in range(heads):
            v_cols = slice(part + head * HEAD_WIDTH, part + (head + 1) * HEAD_WIDTH)
            summed = jnp.dot(
                weights_buf[head],
                jnp.concatenate([kv[slot, ch, :, v_cols] for slot in slots], axis=0),
                preferred_element_type=jnp.float32,
            )
            result = (summed * inverse_buf[head]).astype(o_buf.dtype)
            for j in range(group):
                o_buf[q_at, :, q_cols(head, j)] = result[j * rows : (j + 1) * rows]

    @pl.loop(0, chunks + nz)
    def _(t):
        @pl.when(t < chunks)
        def _():
            local(t, 0).wait()
            local(t, 1).wait()

            @pl.when(normal(t))
            def _():
                remote(0, 2 * nz, t, hop_row, next_line).start()

            @pl.when((z < last) & (jnp.logical_not(moved(t)) | (z < last - 1)))
            def _():
                remote(0, 2, t, fwd_row, up).start()

            @pl.when(moved(t) & (z == last))
            def _():
                remote(0, -2, t, ahead_row, down).start()

            @pl.when(normal(t))
            def _():
                to_partner(0, t)

            @pl.when(moved(t) & (z == last - 1) & (core == 1))
            def _():
                remote(0, -1, t, edge_row, partner).start()

        for d in range(nz, 0, -1):
            ch = t - (nz + 1 - d)

            @pl.when((ch >= 0) & (ch < chunks) & (z < d) & normal(ch))
            def _():
                arrived(2 * d, ch)
                if d > 1:

                    @pl.when((z > 0) & (jnp.logical_not(moved(ch)) | (z > 1)))
                    def _():
                        remote(2 * d, 2 * d - 2, ch, bwd_row + d, down).start()

                to_partner(d, ch)
                if d == nz:

                    @pl.when(moved(ch) & (z == 1) & (core == 0))
                    def _():
                        remote(2 * nz, 2 * nz + 1, ch, edge_row, partner).start()

        for d in range(1, nz):
            ch = t - d

            @pl.when((ch >= 0) & (ch < chunks) & (z >= d) & normal(ch))
            def _():
                arrived(2 * d, ch)
                if d < nz - 1:

                    @pl.when((z < last) & (jnp.logical_not(moved(ch)) | (z < last - 1)))
                    def _():
                        remote(2 * d, 2 * d + 2, ch, fwd_row + d, up).start()

                to_partner(d, ch)
                if d == 1:

                    @pl.when(moved(ch) & (z == 1))
                    def _():
                        remote(2, 2 * nz + 2, ch, far_row, next_line).start()

        before = t - 1

        @pl.when((before >= 0) & (before < chunks) & moved(before))
        def _():
            @pl.when(at_end)
            def _():
                query_copy(before).wait()

            @pl.when(z == 0)
            def _():
                ask(before, up).start()

            @pl.when(z == last)
            def _():
                ask(before, down).start()

            @pl.when(z == last - 1)
            def _():
                arrived(-2, before)
                remote(-2, 2 * nz - 2, before, far_row, next_line).start()

                @pl.when(core == 0)
                def _():
                    remote(-2, -1, before, edge_row, partner).start()

        earlier = t - 2

        @pl.when((earlier >= 0) & (earlier < chunks) & moved(earlier) & (z == 1))
        def _():
            arrived(2 * nz + 2, earlier)

            @pl.when(core == 1)
            def _():
                remote(2 * nz + 2, 2 * nz + 1, earlier, edge_row, partner).start()

        ch = t - nz

        @pl.when((ch >= 0) & normal(ch))
        def _():
            for d in range(nz):
                arrived(2 * d + 1, ch)
            query_copy(ch).wait()
            helps = helper & moved(ch)

            @pl.when(helps)
            def _():
                ask(ch, partner).wait_recv()

                @pl.when(z == 1)
                def _():
                    arrived(2 * nz + 1, ch)

                @pl.when(z == last - 1)
                def _():
                    arrived(-1, ch)

            @pl.loop(jnp.where(helps, 0, 1), 2)
            def _(own):
                other = 1 - own
                attend(
                    ch,
                    other * (chunks + ch // MOVED) + own * ch,
                    other * jnp.where(z == 1, 2, -2),
                )

                @pl.when(other == 1)
                def _():
                    @pl.when(z == 1)
                    def _():
                        answer(ch, down).start()

                    @pl.when(z == last - 1)
                    def _():
                        answer(ch, up).start()

            result_copy(ch).start()

    @pl.loop(0, chunks)
    def _(ch):
        def sent(row):
            remote(0, 1, ch, row, partner).wait_send()

        @pl.when(moved(ch) & at_end)
        def _():
            answer(ch, partner).wait_recv()
            result_copy(ch).start()
            ask(ch, partner).wait_send()

        result_copy(ch).wait()

        @pl.when(moved(ch) & helper)
        def _():
            sent(far_row)
            sent(edge_row)
            answer(ch, partner).wait_send()

        @pl.when(moved(ch) & (z == last))
        def _():
            sent(ahead_row)

        for d in range(nz - 1):

            @pl.when((z >= d) & (z < last) & (jnp.logical_not(moved(ch)) | (z < last - 1)))
            def _():
                sent(fwd_row + d)

        for d in range(2, nz + 1):

            @pl.when((z < d) & (z > 0) & (jnp.logical_not(moved(ch)) | ((z > 1) & (z < last))))
            def _():
                sent(bwd_row + d)

        @pl.when(normal(ch))
        def _():
            sent(hop_row)
            for d in range(nz + 1):
                if d == 0:

                    @pl.when(core == 0)
                    def _():
                        sent(mate_row)

                elif d == nz:

                    @pl.when(core == 1)
                    def _():
                        sent(mate_row + nz)

                else:
                    sent(mate_row + d)


def by_window(n_grp, n_cp, queries, keys, values, doc_lengths):
    streams, rows, _ = queries.shape
    chunks = streams * PARTS
    width = 2 * keys.shape[2] // PARTS
    window = (n_cp + 1) * rows
    nz = n_cp // 2
    pairs = streams * QUERY_HEADS * rows * window
    heads = KEY_VALUE_HEADS // PARTS
    stacked = rows * QUERY_HEADS // KEY_VALUE_HEADS
    held = (chunks + chunks // MOVED, rows, queries.shape[2] // PARTS)
    return pl.pallas_call(
        functools.partial(window_kernel, n_grp, n_cp, streams),
        out_shape=jax.ShapeDtypeStruct(queries.shape, queries.dtype),
        in_specs=[
            pl.BlockSpec(memory_space=pl.ANY),
            pl.BlockSpec(memory_space=pl.ANY),
            pl.BlockSpec(memory_space=pl.ANY),
            pl.BlockSpec(memory_space=pltpu.SMEM),
        ],
        out_specs=pl.BlockSpec(memory_space=pl.ANY),
        scratch_shapes=[
            pltpu.VMEM((n_cp + 1 + 2 * OFF, chunks, rows, width), keys.dtype),
            pltpu.VMEM(held, queries.dtype),
            pltpu.VMEM(held, queries.dtype),
            pltpu.VMEM((rows, window), jnp.float32),
            pltpu.VMEM((heads, stacked, window), jnp.float32),
            pltpu.VMEM((heads, stacked, window), jnp.bfloat16),
            pltpu.VMEM((heads, stacked, HEAD_WIDTH), jnp.float32),
            pltpu.SemaphoreType.DMA((4, chunks)),
            pltpu.SemaphoreType.DMA((3 * nz + 5, chunks)),
            pltpu.SemaphoreType.DMA((n_cp + 3 + 2 * OFF, chunks)),
        ],
        cost_estimate=pl.CostEstimate(
            flops=4 * pairs * HEAD_WIDTH, bytes_accessed=5 * queries.size, transcendentals=pairs
        ),
        compiler_params=pltpu.CompilerParams(
            collective_id=0, has_side_effects=True, vmem_limit_bytes=56 * 2**20
        ),
        name="window_attention",
    )(queries, keys, values, doc_lengths)


def window_fits(n_grp, n_cp, queries, keys):
    line = 2 * keys.shape[0] * keys.shape[1] // n_grp * keys.shape[2] * keys.dtype.itemsize
    return n_cp % 2 == 0 and n_cp >= 8 and n_grp >= 3 and line <= WINDOW_BYTES


def doc_of(positions, ends):
    return jnp.sum((positions[:, None] >= ends[None, :]).astype(jnp.int32), axis=1)


def doc_first(positions, ends):
    return jnp.max(jnp.where(ends[None, :] <= positions[:, None], ends[None, :], 0), axis=1)


def absorb(state, scores, allowed, value_portion):
    running_max, running_sum, running_acc = state
    scores = jnp.where(allowed, scores, NEGATIVE)
    new_max = jnp.maximum(running_max, jnp.max(scores, axis=-1))
    factor = jnp.exp(running_max - new_max)
    probs = jnp.where(allowed, jnp.exp(scores - new_max[..., None]), 0.0)
    new_sum = running_sum * factor + jnp.sum(probs, axis=-1)
    product = jnp.einsum(
        "hqk,khd->hqd",
        probs.astype(jnp.bfloat16),
        value_portion,
        preferred_element_type=jnp.float32,
    )
    return (new_max, new_sum, running_acc * factor[..., None] + product)


def attend_stream(query_seq, key_seq, value_seq, ends):
    stream_len = query_seq.shape[0]
    items = query_seq.shape[1]
    scale = HEAD_WIDTH ** (-0.5)
    positions = jnp.arange(stream_len, dtype=jnp.int32)
    all_docs = doc_of(positions, ends)
    all_firsts = doc_first(positions, ends)
    span = min(512, stream_len)
    spans = stream_len // span

    def query_span(number):
        begin = number * span
        query_tile = lax.dynamic_slice_in_dim(query_seq, begin, span, 0)
        query_pos = lax.dynamic_slice_in_dim(positions, begin, span, 0)
        query_doc = lax.dynamic_slice_in_dim(all_docs, begin, span, 0)
        first_span = lax.dynamic_index_in_dim(all_firsts, begin, 0, keepdims=False) // span

        def key_span(other, state):
            offset = other * span
            key_tile = lax.dynamic_slice_in_dim(key_seq, offset, span, 0)
            value_tile = lax.dynamic_slice_in_dim(value_seq, offset, span, 0)
            key_pos = lax.dynamic_slice_in_dim(positions, offset, span, 0)
            key_doc = lax.dynamic_slice_in_dim(all_docs, offset, span, 0)
            allowed = (key_pos[None, :] <= query_pos[:, None]) & (
                key_doc[None, :] == query_doc[:, None]
            )
            scores = (
                jnp.einsum("qhd,khd->hqk", query_tile, key_tile, preferred_element_type=jnp.float32)
                * scale
            )
            return absorb(state, scores, allowed, value_tile)

        start_state = (
            jnp.full((items, span), NEGATIVE, jnp.float32),
            jnp.zeros((items, span), jnp.float32),
            jnp.zeros((items, span, HEAD_WIDTH), jnp.float32),
        )
        final_max, final_sum, final_acc = lax.fori_loop(
            first_span, number + 1, key_span, start_state
        )
        return (final_acc / final_sum[..., None]).transpose(1, 0, 2).astype(jnp.bfloat16)

    tiles = lax.map(query_span, jnp.arange(spans, dtype=jnp.int32))
    return tiles.reshape(stream_len, items, HEAD_WIDTH)


def on_device(queries, keys, values, doc_lengths):
    n_ranks = lax.axis_size("cp")
    n_streams = queries.shape[0]
    rows_per = queries.shape[1]
    group_count = QUERY_HEADS // KEY_VALUE_HEADS
    per_rank = QUERY_HEADS // n_ranks
    stream_id = lax.axis_index("grp")
    lengths_row = lax.dynamic_index_in_dim(doc_lengths, stream_id, 0, keepdims=False)
    ends = jnp.cumsum(lengths_row)

    def by_heads(array):
        shaped = array.reshape(n_streams, rows_per, n_ranks, per_rank, HEAD_WIDTH)
        return shaped.transpose(0, 2, 1, 3, 4).reshape(
            n_streams * n_ranks, rows_per, per_rank, HEAD_WIDTH
        )

    key_wide = jnp.repeat(
        keys.reshape(n_streams, rows_per, KEY_VALUE_HEADS, HEAD_WIDTH), group_count, axis=2
    )
    value_wide = jnp.repeat(
        values.reshape(n_streams, rows_per, KEY_VALUE_HEADS, HEAD_WIDTH), group_count, axis=2
    )
    query_split = by_heads(queries)
    key_divided_rows = by_heads(key_wide)
    value_divided_rows = by_heads(value_wide)
    query_part = lax.all_to_all(query_split, ("grp", "cp"), split_axis=0, concat_axis=1, tiled=True)
    key_portion = lax.all_to_all(
        key_divided_rows, ("grp", "cp"), split_axis=0, concat_axis=1, tiled=True
    )
    value_portion = lax.all_to_all(
        value_divided_rows, ("grp", "cp"), split_axis=0, concat_axis=1, tiled=True
    )
    outcome = attend_stream(query_part[0], key_portion[0], value_portion[0], ends)
    head_output = outcome[None]
    returned = lax.all_to_all(head_output, ("grp", "cp"), split_axis=1, concat_axis=0, tiled=True)
    shaped = returned.reshape(n_streams, n_ranks, rows_per, per_rank, HEAD_WIDTH).transpose(
        0, 2, 1, 3, 4
    )
    return shaped.reshape(n_streams, rows_per, QUERY_HEADS * HEAD_WIDTH)


def solution(mesh):
    n_grp, n_cp = mesh.shape["grp"], mesh.shape["cp"]
    placed = (
        P(None, ("grp", "cp"), None),
        P(None, ("grp", "cp"), None),
        P(None, ("grp", "cp"), None),
        P(),
    )

    def run(queries, keys, values, doc_lengths):
        if window_fits(n_grp, n_cp, queries, keys):
            plan = functools.partial(by_window, n_grp, n_cp)
        else:
            plan = on_device
        return jax.shard_map(
            plan,
            mesh=mesh,
            in_specs=placed,
            out_specs=P(None, ("grp", "cp"), None),
            check_vma=False,
        )(queries, keys, values, doc_lengths)

    return run
```

```python
import functools

import jax
import jax.numpy as jnp
from jax import lax
from jax.experimental import pallas as pl
from jax.experimental.pallas import tpu as pltpu
from jax.sharding import PartitionSpec as P

MESH = pl.DeviceIdType.MESH
PARTS = 4
MOVED = 2
BLOCK = 32
OFF = 2
WINDOW_BYTES = 40 * 2**20

QUERY_HEADS = 32
KEY_VALUE_HEADS = 8
HEAD_WIDTH = 128
NEGATIVE = -1e30
LOG2_E = 1.4426950408889634


def window_kernel(
    n_grp,
    n_cp,
    streams,
    q_ref,
    k_ref,
    v_ref,
    len_ref,
    o_ref,
    kv,
    q_buf,
    o_buf,
    bias,
    scores_buf,
    weights_buf,
    inverse_buf,
    local_sem,
    send_sem,
    recv_sem,
):
    grp, cp = lax.axis_index("grp"), lax.axis_index("cp")
    z, core = cp // 2, cp % 2
    nz = n_cp // 2
    last = nz - 1
    chunks = streams * PARTS
    rows = k_ref.shape[1]
    part = k_ref.shape[2] // PARTS
    heads = part // HEAD_WIDTH
    group = QUERY_HEADS // KEY_VALUE_HEADS
    wide = part * group
    partner = (grp, z * 2 + 1 - core)
    up = (grp, cp + 2)
    down = (grp, cp - 2)
    next_line = ((grp + 1) % n_grp, cp)
    prev_line = ((grp + n_grp - 1) % n_grp, cp)
    fwd_row, hop_row, bwd_row, mate_row = 0, nz - 1, nz - 2, 2 * nz - 1
    far_row, ahead_row, edge_row, ask_row, answer_row = (3 * nz + i for i in range(5))
    ask_slot, answer_slot = n_cp + 2 * OFF + 1, n_cp + 2 * OFF + 2
    at_end = (z == 0) | (z == last)
    helper = (z == 1) | (z == last - 1)

    def moved(ch):
        return (ch % MOVED == 1) & (ch > MOVED) & (ch < chunks - 1)

    def normal(ch):
        return jnp.logical_not(moved(ch) & at_end)

    def local(ch, which):
        source = (k_ref, v_ref)[which]
        cols = pl.ds(pl.multiple_of((ch % PARTS) * part, part), part)
        return pltpu.make_async_copy(
            source.at[ch // PARTS, :, cols],
            kv.at[OFF, ch, :, pl.ds(which * part, part)],
            local_sem.at[which, ch],
        )

    def own_columns(ch):
        return ch // PARTS, slice(None), pl.ds(pl.multiple_of((ch % PARTS) * wide, wide), wide)

    def query_copy(ch):
        return pltpu.make_async_copy(q_ref.at[own_columns(ch)], q_buf.at[ch], local_sem.at[2, ch])

    def result_copy(ch):
        return pltpu.make_async_copy(o_buf.at[ch], o_ref.at[own_columns(ch)], local_sem.at[3, ch])

    def remote(source, target, ch, row, device):
        return pltpu.make_async_remote_copy(
            src_ref=kv.at[OFF + source, ch],
            dst_ref=kv.at[OFF + target, ch],
            send_sem=send_sem.at[row, ch],
            recv_sem=recv_sem.at[OFF + target, ch],
            device_id=device,
            device_id_type=MESH,
        )

    def arrived(slot, ch):
        remote(slot, slot, ch, 0, partner).wait_recv()

    def ask(ch, device):
        return pltpu.make_async_remote_copy(
            src_ref=q_buf.at[ch],
            dst_ref=q_buf.at[chunks + ch // MOVED],
            send_sem=send_sem.at[ask_row, ch],
            recv_sem=recv_sem.at[ask_slot, ch],
            device_id=device,
            device_id_type=MESH,
        )

    def answer(ch, device):
        return pltpu.make_async_remote_copy(
            src_ref=o_buf.at[chunks + ch // MOVED],
            dst_ref=o_buf.at[ch],
            send_sem=send_sem.at[answer_row, ch],
            recv_sem=recv_sem.at[answer_slot, ch],
            device_id=device,
            device_id_type=MESH,
        )

    @pl.loop(0, chunks)
    def _(ch):
        local(ch, 0).start()
        local(ch, 1).start()

    @pl.loop(0, chunks)
    def _(ch):
        query_copy(ch).start()

    barrier = pltpu.get_barrier_semaphore()

    def greet(device):
        pl.semaphore_signal(barrier, inc=1, device_id=device, device_id_type=MESH)

    greet(partner)
    greet(next_line)
    greet(prev_line)

    @pl.when(z < last)
    def _():
        greet(up)

    @pl.when(z > 0)
    def _():
        greet(down)

    pl.semaphore_wait(barrier, jnp.where(at_end, 4, 5))

    def to_partner(d, ch):
        if d < nz:

            @pl.when(core == 0)
            def _():
                remote(2 * d, 2 * d + 1, ch, mate_row + d, partner).start()

        if d > 0:

            @pl.when(core == 1)
            def _():
                remote(2 * d, 2 * d - 1, ch, mate_row + d, partner).start()

    def attend(ch, q_at, shift):
        stream = ch // PARTS
        base = (grp * n_cp + cp - shift) * rows
        row = lax.broadcasted_iota(jnp.int32, (rows, rows), 0)
        lane = lax.broadcasted_iota(jnp.int32, (rows, rows), 1)
        first = jnp.zeros((rows, rows), jnp.int32)
        end = jnp.int32(0)
        for doc in range(len_ref.shape[1]):
            end = end + len_ref[stream, doc]
            first = jnp.maximum(first, jnp.where(row + base >= end, end, 0))
        for r in range(n_cp + 1):
            allowed = lane + (base - r * rows) >= first
            if r == 0:
                allowed = allowed & (lane <= row)
            bias[:, r * rows : (r + 1) * rows] = jnp.where(allowed, 0.0, NEGATIVE)

        slots = [OFF + shift + r for r in range(n_cp + 1)]

        def q_cols(head, j):
            at = (head * group + j) * HEAD_WIDTH
            return slice(at, at + HEAD_WIDTH)

        for head in range(heads):
            k_cols = slice(head * HEAD_WIDTH, (head + 1) * HEAD_WIDTH)
            scores_buf[head] = lax.dot_general(
                jnp.concatenate([q_buf[q_at, :, q_cols(head, j)] for j in range(group)], axis=0),
                jnp.concatenate([kv[slot, ch, :, k_cols] for slot in slots], axis=0),
                (((1,), (1,)), ((), ())),
                preferred_element_type=jnp.float32,
            )

        def normalise(i, carry):
            at = pl.ds(pl.multiple_of(i * BLOCK, BLOCK), BLOCK)
            token = pl.ds(pl.multiple_of(i % (rows // BLOCK) * BLOCK, BLOCK), BLOCK)
            mask = bias[token, :]
            for head in range(heads):
                scores = scores_buf[head, at, :] + mask
                largest = jnp.max(scores, axis=1, keepdims=True)
                probs = jnp.exp2((scores - largest) * (HEAD_WIDTH**-0.5 * LOG2_E))
                total = jnp.sum(probs, axis=1, keepdims=True)
                weights_buf[head, at, :] = probs.astype(jnp.bfloat16)
                inverse_buf[head, at, :] = jnp.broadcast_to(1.0 / total, (BLOCK, HEAD_WIDTH))
            return carry

        lax.fori_loop(0, group * rows // BLOCK, normalise, 0, unroll=2)

        for head in range(heads):
            v_cols = slice(part + head * HEAD_WIDTH, part + (head + 1) * HEAD_WIDTH)
            summed = jnp.dot(
                weights_buf[head],
                jnp.concatenate([kv[slot, ch, :, v_cols] for slot in slots], axis=0),
                preferred_element_type=jnp.float32,
            )
            result = (summed * inverse_buf[head]).astype(o_buf.dtype)
            for j in range(group):
                o_buf[q_at, :, q_cols(head, j)] = result[j * rows : (j + 1) * rows]

    def ahead(ch):
        local(ch, 0).wait()
        local(ch, 1).wait()

        @pl.when(normal(ch))
        def _():
            remote(0, 2 * nz, ch, hop_row, next_line).start()

        @pl.when(moved(ch) & (z == last))
        def _():
            remote(0, -2, ch, ahead_row, down).start()

    ahead(0)

    @pl.loop(0, chunks + nz - 1)
    def _(t):
        @pl.when(t < chunks)
        def _():
            @pl.when((z < last) & (jnp.logical_not(moved(t)) | (z < last - 1)))
            def _():
                remote(0, 2, t, fwd_row, up).start()

            @pl.when(normal(t))
            def _():
                to_partner(0, t)

            @pl.when(moved(t) & (z == last - 1) & (core == 1))
            def _():
                remote(0, -1, t, edge_row, partner).start()

        @pl.when(t + 1 < chunks)
        def _():
            ahead(t + 1)

        for d in range(nz, 0, -1):
            ch = t - (nz - d)

            @pl.when((ch >= 0) & (ch < chunks) & (z < d) & normal(ch))
            def _():
                arrived(2 * d, ch)
                if d > 1:

                    @pl.when((z > 0) & (jnp.logical_not(moved(ch)) | (z > 1)))
                    def _():
                        remote(2 * d, 2 * d - 2, ch, bwd_row + d, down).start()

                to_partner(d, ch)
                if d == nz:

                    @pl.when(moved(ch) & (z == 1) & (core == 0))
                    def _():
                        remote(2 * nz, 2 * nz + 1, ch, edge_row, partner).start()

        for d in range(1, nz):
            ch = t - d

            @pl.when((ch >= 0) & (ch < chunks) & (z >= d) & normal(ch))
            def _():
                arrived(2 * d, ch)
                if d < nz - 1:

                    @pl.when((z < last) & (jnp.logical_not(moved(ch)) | (z < last - 1)))
                    def _():
                        remote(2 * d, 2 * d + 2, ch, fwd_row + d, up).start()

                to_partner(d, ch)
                if d == 1:

                    @pl.when(moved(ch) & (z == 1))
                    def _():
                        remote(2, 2 * nz + 2, ch, far_row, next_line).start()

        before = t - 1

        @pl.when((before >= 0) & (before < chunks) & moved(before))
        def _():
            @pl.when(at_end)
            def _():
                query_copy(before).wait()

            @pl.when(z == 0)
            def _():
                ask(before, up).start()

            @pl.when(z == last)
            def _():
                ask(before, down).start()

        @pl.when((t < chunks) & moved(t) & (z == last - 1))
        def _():
            arrived(-2, t)
            remote(-2, 2 * nz - 2, t, far_row, next_line).start()

            @pl.when(core == 0)
            def _():
                remote(-2, -1, t, edge_row, partner).start()

        earlier = t - 2

        @pl.when((earlier >= 0) & (earlier < chunks) & moved(earlier) & (z == 1))
        def _():
            arrived(2 * nz + 2, earlier)

            @pl.when(core == 1)
            def _():
                remote(2 * nz + 2, 2 * nz + 1, earlier, edge_row, partner).start()

        ch = t - (nz - 1)

        @pl.when((ch >= 0) & normal(ch))
        def _():
            for d in range(nz):
                arrived(2 * d + 1, ch)
            query_copy(ch).wait()
            helps = helper & moved(ch)

            @pl.when(helps)
            def _():
                ask(ch, partner).wait_recv()

                @pl.when(z == 1)
                def _():
                    arrived(2 * nz + 1, ch)

                @pl.when(z == last - 1)
                def _():
                    arrived(-1, ch)

            @pl.loop(jnp.where(helps, 0, 1), 2)
            def _(own):
                other = 1 - own
                attend(
                    ch,
                    other * (chunks + ch // MOVED) + own * ch,
                    other * jnp.where(z == 1, 2, -2),
                )

                @pl.when(other == 1)
                def _():
                    @pl.when(z == 1)
                    def _():
                        answer(ch, down).start()

                    @pl.when(z == last - 1)
                    def _():
                        answer(ch, up).start()

            result_copy(ch).start()

    @pl.loop(0, chunks)
    def _(ch):
        def sent(row):
            remote(0, 1, ch, row, partner).wait_send()

        @pl.when(moved(ch) & at_end)
        def _():
            answer(ch, partner).wait_recv()
            result_copy(ch).start()
            ask(ch, partner).wait_send()

        result_copy(ch).wait()

        @pl.when(moved(ch) & helper)
        def _():
            sent(far_row)
            sent(edge_row)
            answer(ch, partner).wait_send()

        @pl.when(moved(ch) & (z == last))
        def _():
            sent(ahead_row)

        for d in range(nz - 1):

            @pl.when((z >= d) & (z < last) & (jnp.logical_not(moved(ch)) | (z < last - 1)))
            def _():
                sent(fwd_row + d)

        for d in range(2, nz + 1):

            @pl.when((z < d) & (z > 0) & (jnp.logical_not(moved(ch)) | ((z > 1) & (z < last))))
            def _():
                sent(bwd_row + d)

        @pl.when(normal(ch))
        def _():
            sent(hop_row)
            for d in range(nz + 1):
                if d == 0:

                    @pl.when(core == 0)
                    def _():
                        sent(mate_row)

                elif d == nz:

                    @pl.when(core == 1)
                    def _():
                        sent(mate_row + nz)

                else:
                    sent(mate_row + d)


def by_window(n_grp, n_cp, queries, keys, values, doc_lengths):
    streams, rows, _ = queries.shape
    chunks = streams * PARTS
    width = 2 * keys.shape[2] // PARTS
    window = (n_cp + 1) * rows
    nz = n_cp // 2
    pairs = streams * QUERY_HEADS * rows * window
    heads = KEY_VALUE_HEADS // PARTS
    stacked = rows * QUERY_HEADS // KEY_VALUE_HEADS
    held = (chunks + chunks // MOVED, rows, queries.shape[2] // PARTS)
    return pl.pallas_call(
        functools.partial(window_kernel, n_grp, n_cp, streams),
        out_shape=jax.ShapeDtypeStruct(queries.shape, queries.dtype),
        in_specs=[
            pl.BlockSpec(memory_space=pl.ANY),
            pl.BlockSpec(memory_space=pl.ANY),
            pl.BlockSpec(memory_space=pl.ANY),
            pl.BlockSpec(memory_space=pltpu.SMEM),
        ],
        out_specs=pl.BlockSpec(memory_space=pl.ANY),
        scratch_shapes=[
            pltpu.VMEM((n_cp + 1 + 2 * OFF, chunks, rows, width), keys.dtype),
            pltpu.VMEM(held, queries.dtype),
            pltpu.VMEM(held, queries.dtype),
            pltpu.VMEM((rows, window), jnp.float32),
            pltpu.VMEM((heads, stacked, window), jnp.float32),
            pltpu.VMEM((heads, stacked, window), jnp.bfloat16),
            pltpu.VMEM((heads, stacked, HEAD_WIDTH), jnp.float32),
            pltpu.SemaphoreType.DMA((4, chunks)),
            pltpu.SemaphoreType.DMA((3 * nz + 5, chunks)),
            pltpu.SemaphoreType.DMA((n_cp + 3 + 2 * OFF, chunks)),
        ],
        cost_estimate=pl.CostEstimate(
            flops=4 * pairs * HEAD_WIDTH, bytes_accessed=5 * queries.size, transcendentals=pairs
        ),
        compiler_params=pltpu.CompilerParams(
            collective_id=0, has_side_effects=True, vmem_limit_bytes=56 * 2**20
        ),
        name="window_attention",
    )(queries, keys, values, doc_lengths)


def window_fits(n_grp, n_cp, queries, keys):
    line = 2 * keys.shape[0] * keys.shape[1] // n_grp * keys.shape[2] * keys.dtype.itemsize
    return n_cp % 2 == 0 and n_cp >= 8 and n_grp >= 3 and line <= WINDOW_BYTES


def doc_of(positions, ends):
    return jnp.sum((positions[:, None] >= ends[None, :]).astype(jnp.int32), axis=1)


def doc_first(positions, ends):
    return jnp.max(jnp.where(ends[None, :] <= positions[:, None], ends[None, :], 0), axis=1)


def absorb(state, scores, allowed, value_portion):
    running_max, running_sum, running_acc = state
    scores = jnp.where(allowed, scores, NEGATIVE)
    new_max = jnp.maximum(running_max, jnp.max(scores, axis=-1))
    factor = jnp.exp(running_max - new_max)
    probs = jnp.where(allowed, jnp.exp(scores - new_max[..., None]), 0.0)
    new_sum = running_sum * factor + jnp.sum(probs, axis=-1)
    product = jnp.einsum(
        "hqk,khd->hqd",
        probs.astype(jnp.bfloat16),
        value_portion,
        preferred_element_type=jnp.float32,
    )
    return (new_max, new_sum, running_acc * factor[..., None] + product)


def attend_stream(query_seq, key_seq, value_seq, ends):
    stream_len = query_seq.shape[0]
    items = query_seq.shape[1]
    scale = HEAD_WIDTH ** (-0.5)
    positions = jnp.arange(stream_len, dtype=jnp.int32)
    all_docs = doc_of(positions, ends)
    all_firsts = doc_first(positions, ends)
    span = min(512, stream_len)
    spans = stream_len // span

    def query_span(number):
        begin = number * span
        query_tile = lax.dynamic_slice_in_dim(query_seq, begin, span, 0)
        query_pos = lax.dynamic_slice_in_dim(positions, begin, span, 0)
        query_doc = lax.dynamic_slice_in_dim(all_docs, begin, span, 0)
        first_span = lax.dynamic_index_in_dim(all_firsts, begin, 0, keepdims=False) // span

        def key_span(other, state):
            offset = other * span
            key_tile = lax.dynamic_slice_in_dim(key_seq, offset, span, 0)
            value_tile = lax.dynamic_slice_in_dim(value_seq, offset, span, 0)
            key_pos = lax.dynamic_slice_in_dim(positions, offset, span, 0)
            key_doc = lax.dynamic_slice_in_dim(all_docs, offset, span, 0)
            allowed = (key_pos[None, :] <= query_pos[:, None]) & (
                key_doc[None, :] == query_doc[:, None]
            )
            scores = (
                jnp.einsum("qhd,khd->hqk", query_tile, key_tile, preferred_element_type=jnp.float32)
                * scale
            )
            return absorb(state, scores, allowed, value_tile)

        start_state = (
            jnp.full((items, span), NEGATIVE, jnp.float32),
            jnp.zeros((items, span), jnp.float32),
            jnp.zeros((items, span, HEAD_WIDTH), jnp.float32),
        )
        final_max, final_sum, final_acc = lax.fori_loop(
            first_span, number + 1, key_span, start_state
        )
        return (final_acc / final_sum[..., None]).transpose(1, 0, 2).astype(jnp.bfloat16)

    tiles = lax.map(query_span, jnp.arange(spans, dtype=jnp.int32))
    return tiles.reshape(stream_len, items, HEAD_WIDTH)


def on_device(queries, keys, values, doc_lengths):
    n_ranks = lax.axis_size("cp")
    n_streams = queries.shape[0]
    rows_per = queries.shape[1]
    group_count = QUERY_HEADS // KEY_VALUE_HEADS
    per_rank = QUERY_HEADS // n_ranks
    stream_id = lax.axis_index("grp")
    lengths_row = lax.dynamic_index_in_dim(doc_lengths, stream_id, 0, keepdims=False)
    ends = jnp.cumsum(lengths_row)

    def by_heads(array):
        shaped = array.reshape(n_streams, rows_per, n_ranks, per_rank, HEAD_WIDTH)
        return shaped.transpose(0, 2, 1, 3, 4).reshape(
            n_streams * n_ranks, rows_per, per_rank, HEAD_WIDTH
        )

    key_wide = jnp.repeat(
        keys.reshape(n_streams, rows_per, KEY_VALUE_HEADS, HEAD_WIDTH), group_count, axis=2
    )
    value_wide = jnp.repeat(
        values.reshape(n_streams, rows_per, KEY_VALUE_HEADS, HEAD_WIDTH), group_count, axis=2
    )
    query_split = by_heads(queries)
    key_divided_rows = by_heads(key_wide)
    value_divided_rows = by_heads(value_wide)
    query_part = lax.all_to_all(query_split, ("grp", "cp"), split_axis=0, concat_axis=1, tiled=True)
    key_portion = lax.all_to_all(
        key_divided_rows, ("grp", "cp"), split_axis=0, concat_axis=1, tiled=True
    )
    value_portion = lax.all_to_all(
        value_divided_rows, ("grp", "cp"), split_axis=0, concat_axis=1, tiled=True
    )
    outcome = attend_stream(query_part[0], key_portion[0], value_portion[0], ends)
    head_output = outcome[None]
    returned = lax.all_to_all(head_output, ("grp", "cp"), split_axis=1, concat_axis=0, tiled=True)
    shaped = returned.reshape(n_streams, n_ranks, rows_per, per_rank, HEAD_WIDTH).transpose(
        0, 2, 1, 3, 4
    )
    return shaped.reshape(n_streams, rows_per, QUERY_HEADS * HEAD_WIDTH)


def solution(mesh):
    n_grp, n_cp = mesh.shape["grp"], mesh.shape["cp"]
    placed = (
        P(None, ("grp", "cp"), None),
        P(None, ("grp", "cp"), None),
        P(None, ("grp", "cp"), None),
        P(),
    )

    def run(queries, keys, values, doc_lengths):
        if window_fits(n_grp, n_cp, queries, keys):
            plan = functools.partial(by_window, n_grp, n_cp)
        else:
            plan = on_device
        return jax.shard_map(
            plan,
            mesh=mesh,
            in_specs=placed,
            out_specs=P(None, ("grp", "cp"), None),
            check_vma=False,
        )(queries, keys, values, doc_lengths)

    return run
```

```python
import functools

import jax
import jax.numpy as jnp
from jax import lax
from jax.experimental import pallas as pl
from jax.experimental.pallas import tpu as pltpu
from jax.sharding import PartitionSpec as P

MESH = pl.DeviceIdType.MESH
PARTS = 4
MOVED = 2
BLOCK = 32
OFF = 2
WINDOW_BYTES = 40 * 2**20

QUERY_HEADS = 32
KEY_VALUE_HEADS = 8
HEAD_WIDTH = 128
NEGATIVE = -1e30
LOG2_E = 1.4426950408889634


def window_kernel(
    n_grp,
    n_cp,
    streams,
    q_ref,
    k_ref,
    v_ref,
    len_ref,
    o_ref,
    kv,
    q_buf,
    o_buf,
    bias,
    scores_buf,
    weights_buf,
    inverse_buf,
    local_sem,
    send_sem,
    recv_sem,
):
    grp, cp = lax.axis_index("grp"), lax.axis_index("cp")
    z, core = cp // 2, cp % 2
    nz = n_cp // 2
    last = nz - 1
    chunks = streams * PARTS
    rows = k_ref.shape[1]
    part = k_ref.shape[2] // PARTS
    heads = part // HEAD_WIDTH
    group = QUERY_HEADS // KEY_VALUE_HEADS
    wide = part * group
    partner = (grp, z * 2 + 1 - core)
    up = (grp, cp + 2)
    down = (grp, cp - 2)
    next_line = ((grp + 1) % n_grp, cp)
    prev_line = ((grp + n_grp - 1) % n_grp, cp)
    fwd_row, hop_row, bwd_row, mate_row = 0, nz - 1, nz - 2, 2 * nz - 1
    far_row, ahead_row, edge_row, ask_row, answer_row = (3 * nz + i for i in range(5))
    ask_slot, answer_slot = n_cp + 2 * OFF + 1, n_cp + 2 * OFF + 2
    at_end = (z == 0) | (z == last)
    helper = (z == 1) | (z == last - 1)

    def moved(ch):
        return (ch % MOVED == 0) & (ch > 0)

    def normal(ch):
        return jnp.logical_not(moved(ch) & at_end)

    def local(ch, which):
        source = (k_ref, v_ref)[which]
        cols = pl.ds(pl.multiple_of((ch % PARTS) * part, part), part)
        return pltpu.make_async_copy(
            source.at[ch // PARTS, :, cols],
            kv.at[OFF, ch, :, pl.ds(which * part, part)],
            local_sem.at[which, ch],
        )

    def own_columns(ch):
        return ch // PARTS, slice(None), pl.ds(pl.multiple_of((ch % PARTS) * wide, wide), wide)

    def query_copy(ch):
        return pltpu.make_async_copy(q_ref.at[own_columns(ch)], q_buf.at[ch], local_sem.at[2, ch])

    def result_copy(ch):
        return pltpu.make_async_copy(o_buf.at[ch], o_ref.at[own_columns(ch)], local_sem.at[3, ch])

    def remote(source, target, ch, row, device):
        return pltpu.make_async_remote_copy(
            src_ref=kv.at[OFF + source, ch],
            dst_ref=kv.at[OFF + target, ch],
            send_sem=send_sem.at[row, ch],
            recv_sem=recv_sem.at[OFF + target, ch],
            device_id=device,
            device_id_type=MESH,
        )

    def arrived(slot, ch):
        remote(slot, slot, ch, 0, partner).wait_recv()

    def ask(ch, device):
        return pltpu.make_async_remote_copy(
            src_ref=q_buf.at[ch],
            dst_ref=q_buf.at[chunks + ch // MOVED],
            send_sem=send_sem.at[ask_row, ch],
            recv_sem=recv_sem.at[ask_slot, ch],
            device_id=device,
            device_id_type=MESH,
        )

    def answer(ch, device):
        return pltpu.make_async_remote_copy(
            src_ref=o_buf.at[chunks + ch // MOVED],
            dst_ref=o_buf.at[ch],
            send_sem=send_sem.at[answer_row, ch],
            recv_sem=recv_sem.at[answer_slot, ch],
            device_id=device,
            device_id_type=MESH,
        )

    @pl.loop(0, chunks)
    def _(ch):
        local(ch, 0).start()
        local(ch, 1).start()

    @pl.loop(0, chunks)
    def _(ch):
        query_copy(ch).start()

    barrier = pltpu.get_barrier_semaphore()

    def greet(device):
        pl.semaphore_signal(barrier, inc=1, device_id=device, device_id_type=MESH)

    greet(partner)
    greet(next_line)
    greet(prev_line)

    @pl.when(z < last)
    def _():
        greet(up)

    @pl.when(z > 0)
    def _():
        greet(down)

    pl.semaphore_wait(barrier, jnp.where(at_end, 4, 5))

    def to_partner(d, ch):
        if d < nz:

            @pl.when(core == 0)
            def _():
                remote(2 * d, 2 * d + 1, ch, mate_row + d, partner).start()

        if d > 0:

            @pl.when(core == 1)
            def _():
                remote(2 * d, 2 * d - 1, ch, mate_row + d, partner).start()

    def attend(ch, q_at, shift):
        stream = ch // PARTS
        base = (grp * n_cp + cp - shift) * rows
        row = lax.broadcasted_iota(jnp.int32, (rows, rows), 0)
        lane = lax.broadcasted_iota(jnp.int32, (rows, rows), 1)
        first = jnp.zeros((rows, rows), jnp.int32)
        end = jnp.int32(0)
        for doc in range(len_ref.shape[1]):
            end = end + len_ref[stream, doc]
            first = jnp.maximum(first, jnp.where(row + base >= end, end, 0))
        for r in range(n_cp + 1):
            allowed = lane + (base - r * rows) >= first
            if r == 0:
                allowed = allowed & (lane <= row)
            bias[:, r * rows : (r + 1) * rows] = jnp.where(allowed, 0.0, NEGATIVE)

        slots = [OFF + shift + r for r in range(n_cp + 1)]

        def q_cols(head, j):
            at = (head * group + j) * HEAD_WIDTH
            return slice(at, at + HEAD_WIDTH)

        for head in range(heads):
            k_cols = slice(head * HEAD_WIDTH, (head + 1) * HEAD_WIDTH)
            scores_buf[head] = lax.dot_general(
                jnp.concatenate([q_buf[q_at, :, q_cols(head, j)] for j in range(group)], axis=0),
                jnp.concatenate([kv[slot, ch, :, k_cols] for slot in slots], axis=0),
                (((1,), (1,)), ((), ())),
                preferred_element_type=jnp.float32,
            )

        def normalise(i, carry):
            at = pl.ds(pl.multiple_of(i * BLOCK, BLOCK), BLOCK)
            token = pl.ds(pl.multiple_of(i % (rows // BLOCK) * BLOCK, BLOCK), BLOCK)
            mask = bias[token, :]
            for head in range(heads):
                scores = scores_buf[head, at, :] + mask
                largest = jnp.max(scores, axis=1, keepdims=True)
                probs = jnp.exp2((scores - largest) * (HEAD_WIDTH**-0.5 * LOG2_E))
                total = jnp.sum(probs, axis=1, keepdims=True)
                weights_buf[head, at, :] = probs.astype(jnp.bfloat16)
                inverse_buf[head, at, :] = jnp.broadcast_to(1.0 / total, (BLOCK, HEAD_WIDTH))
            return carry

        lax.fori_loop(0, group * rows // BLOCK, normalise, 0, unroll=2)

        for head in range(heads):
            v_cols = slice(part + head * HEAD_WIDTH, part + (head + 1) * HEAD_WIDTH)
            summed = jnp.dot(
                weights_buf[head],
                jnp.concatenate([kv[slot, ch, :, v_cols] for slot in slots], axis=0),
                preferred_element_type=jnp.float32,
            )
            result = (summed * inverse_buf[head]).astype(o_buf.dtype)
            for j in range(group):
                o_buf[q_at, :, q_cols(head, j)] = result[j * rows : (j + 1) * rows]

    def ahead(ch):
        local(ch, 0).wait()
        local(ch, 1).wait()

        @pl.when(normal(ch))
        def _():
            remote(0, 2 * nz, ch, hop_row, next_line).start()

        @pl.when(moved(ch) & (z == last))
        def _():
            remote(0, -2, ch, ahead_row, down).start()

    ahead(0)

    @pl.loop(0, chunks + nz)
    def _(t):
        @pl.when(t < chunks)
        def _():
            @pl.when((z < last) & (jnp.logical_not(moved(t)) | (z < last - 1)))
            def _():
                remote(0, 2, t, fwd_row, up).start()

            @pl.when(normal(t))
            def _():
                to_partner(0, t)

            @pl.when(moved(t) & (z == last - 1) & (core == 1))
            def _():
                remote(0, -1, t, edge_row, partner).start()

        @pl.when(t + 1 < chunks)
        def _():
            ahead(t + 1)

        for d in range(nz, 0, -1):
            ch = t - (nz - d)

            @pl.when((ch >= 0) & (ch < chunks) & (z < d) & normal(ch))
            def _():
                arrived(2 * d, ch)
                if d > 1:

                    @pl.when((z > 0) & (jnp.logical_not(moved(ch)) | (z > 1)))
                    def _():
                        remote(2 * d, 2 * d - 2, ch, bwd_row + d, down).start()

                to_partner(d, ch)
                if d == nz:

                    @pl.when(moved(ch) & (z == 1) & (core == 0))
                    def _():
                        remote(2 * nz, 2 * nz + 1, ch, edge_row, partner).start()

        for d in range(1, nz):
            ch = t - d

            @pl.when((ch >= 0) & (ch < chunks) & (z >= d) & normal(ch))
            def _():
                arrived(2 * d, ch)
                if d < nz - 1:

                    @pl.when((z < last) & (jnp.logical_not(moved(ch)) | (z < last - 1)))
                    def _():
                        remote(2 * d, 2 * d + 2, ch, fwd_row + d, up).start()

                to_partner(d, ch)
                if d == 1:

                    @pl.when(moved(ch) & (z == 1))
                    def _():
                        remote(2, 2 * nz + 2, ch, far_row, next_line).start()

        before = t - 2

        @pl.when((before >= 0) & (before < chunks) & moved(before))
        def _():
            @pl.when(at_end)
            def _():
                query_copy(before).wait()

            @pl.when(z == 0)
            def _():
                ask(before, up).start()

            @pl.when(z == last)
            def _():
                ask(before, down).start()

        @pl.when((t < chunks) & moved(t) & (z == last - 1))
        def _():
            arrived(-2, t)
            remote(-2, 2 * nz - 2, t, far_row, next_line).start()

            @pl.when(core == 0)
            def _():
                remote(-2, -1, t, edge_row, partner).start()

        earlier = t - 2

        @pl.when((earlier >= 0) & (earlier < chunks) & moved(earlier) & (z == 1))
        def _():
            arrived(2 * nz + 2, earlier)

            @pl.when(core == 1)
            def _():
                remote(2 * nz + 2, 2 * nz + 1, earlier, edge_row, partner).start()

        mine, theirs = t - (nz - 1), t - nz
        attends = (mine >= 0) & (mine < chunks) & normal(mine)
        helps = (theirs >= 0) & helper & moved(theirs)

        @pl.loop(jnp.where(helps, 0, 1), jnp.where(attends, 2, 1))
        def _(own):
            other = 1 - own
            ch = theirs + own

            @pl.when(own == 1)
            def _():
                for d in range(nz):
                    arrived(2 * d + 1, ch)
                query_copy(ch).wait()

            @pl.when(other == 1)
            def _():
                ask(ch, partner).wait_recv()

                @pl.when(z == 1)
                def _():
                    arrived(2 * nz + 1, ch)

                @pl.when(z == last - 1)
                def _():
                    arrived(-1, ch)

            attend(
                ch,
                other * (chunks + ch // MOVED) + own * ch,
                other * jnp.where(z == 1, 2, -2),
            )

            @pl.when(own == 1)
            def _():
                result_copy(ch).start()

            @pl.when((other == 1) & (z == 1))
            def _():
                answer(ch, down).start()

            @pl.when((other == 1) & (z == last - 1))
            def _():
                answer(ch, up).start()

    @pl.loop(0, chunks)
    def _(ch):
        def sent(row):
            remote(0, 1, ch, row, partner).wait_send()

        @pl.when(moved(ch) & at_end)
        def _():
            answer(ch, partner).wait_recv()
            result_copy(ch).start()
            ask(ch, partner).wait_send()

        result_copy(ch).wait()

        @pl.when(moved(ch) & helper)
        def _():
            sent(far_row)
            sent(edge_row)
            answer(ch, partner).wait_send()

        @pl.when(moved(ch) & (z == last))
        def _():
            sent(ahead_row)

        for d in range(nz - 1):

            @pl.when((z >= d) & (z < last) & (jnp.logical_not(moved(ch)) | (z < last - 1)))
            def _():
                sent(fwd_row + d)

        for d in range(2, nz + 1):

            @pl.when((z < d) & (z > 0) & (jnp.logical_not(moved(ch)) | ((z > 1) & (z < last))))
            def _():
                sent(bwd_row + d)

        @pl.when(normal(ch))
        def _():
            sent(hop_row)
            for d in range(nz + 1):
                if d == 0:

                    @pl.when(core == 0)
                    def _():
                        sent(mate_row)

                elif d == nz:

                    @pl.when(core == 1)
                    def _():
                        sent(mate_row + nz)

                else:
                    sent(mate_row + d)


def by_window(n_grp, n_cp, queries, keys, values, doc_lengths):
    streams, rows, _ = queries.shape
    chunks = streams * PARTS
    width = 2 * keys.shape[2] // PARTS
    window = (n_cp + 1) * rows
    nz = n_cp // 2
    pairs = streams * QUERY_HEADS * rows * window
    heads = KEY_VALUE_HEADS // PARTS
    stacked = rows * QUERY_HEADS // KEY_VALUE_HEADS
    held = (chunks + chunks // MOVED, rows, queries.shape[2] // PARTS)
    return pl.pallas_call(
        functools.partial(window_kernel, n_grp, n_cp, streams),
        out_shape=jax.ShapeDtypeStruct(queries.shape, queries.dtype),
        in_specs=[
            pl.BlockSpec(memory_space=pl.ANY),
            pl.BlockSpec(memory_space=pl.ANY),
            pl.BlockSpec(memory_space=pl.ANY),
            pl.BlockSpec(memory_space=pltpu.SMEM),
        ],
        out_specs=pl.BlockSpec(memory_space=pl.ANY),
        scratch_shapes=[
            pltpu.VMEM((n_cp + 1 + 2 * OFF, chunks, rows, width), keys.dtype),
            pltpu.VMEM(held, queries.dtype),
            pltpu.VMEM(held, queries.dtype),
            pltpu.VMEM((rows, window), jnp.float32),
            pltpu.VMEM((heads, stacked, window), jnp.float32),
            pltpu.VMEM((heads, stacked, window), jnp.bfloat16),
            pltpu.VMEM((heads, stacked, HEAD_WIDTH), jnp.float32),
            pltpu.SemaphoreType.DMA((4, chunks)),
            pltpu.SemaphoreType.DMA((3 * nz + 5, chunks)),
            pltpu.SemaphoreType.DMA((n_cp + 3 + 2 * OFF, chunks)),
        ],
        cost_estimate=pl.CostEstimate(
            flops=4 * pairs * HEAD_WIDTH, bytes_accessed=5 * queries.size, transcendentals=pairs
        ),
        compiler_params=pltpu.CompilerParams(
            collective_id=0, has_side_effects=True, vmem_limit_bytes=56 * 2**20
        ),
        name="window_attention",
    )(queries, keys, values, doc_lengths)


def window_fits(n_grp, n_cp, queries, keys):
    line = 2 * keys.shape[0] * keys.shape[1] // n_grp * keys.shape[2] * keys.dtype.itemsize
    return n_cp % 2 == 0 and n_cp >= 8 and n_grp >= 3 and line <= WINDOW_BYTES


def doc_of(positions, ends):
    return jnp.sum((positions[:, None] >= ends[None, :]).astype(jnp.int32), axis=1)


def doc_first(positions, ends):
    return jnp.max(jnp.where(ends[None, :] <= positions[:, None], ends[None, :], 0), axis=1)


def absorb(state, scores, allowed, value_portion):
    running_max, running_sum, running_acc = state
    scores = jnp.where(allowed, scores, NEGATIVE)
    new_max = jnp.maximum(running_max, jnp.max(scores, axis=-1))
    factor = jnp.exp(running_max - new_max)
    probs = jnp.where(allowed, jnp.exp(scores - new_max[..., None]), 0.0)
    new_sum = running_sum * factor + jnp.sum(probs, axis=-1)
    product = jnp.einsum(
        "hqk,khd->hqd",
        probs.astype(jnp.bfloat16),
        value_portion,
        preferred_element_type=jnp.float32,
    )
    return (new_max, new_sum, running_acc * factor[..., None] + product)


def attend_stream(query_seq, key_seq, value_seq, ends):
    stream_len = query_seq.shape[0]
    items = query_seq.shape[1]
    scale = HEAD_WIDTH ** (-0.5)
    positions = jnp.arange(stream_len, dtype=jnp.int32)
    all_docs = doc_of(positions, ends)
    all_firsts = doc_first(positions, ends)
    span = min(512, stream_len)
    spans = stream_len // span

    def query_span(number):
        begin = number * span
        query_tile = lax.dynamic_slice_in_dim(query_seq, begin, span, 0)
        query_pos = lax.dynamic_slice_in_dim(positions, begin, span, 0)
        query_doc = lax.dynamic_slice_in_dim(all_docs, begin, span, 0)
        first_span = lax.dynamic_index_in_dim(all_firsts, begin, 0, keepdims=False) // span

        def key_span(other, state):
            offset = other * span
            key_tile = lax.dynamic_slice_in_dim(key_seq, offset, span, 0)
            value_tile = lax.dynamic_slice_in_dim(value_seq, offset, span, 0)
            key_pos = lax.dynamic_slice_in_dim(positions, offset, span, 0)
            key_doc = lax.dynamic_slice_in_dim(all_docs, offset, span, 0)
            allowed = (key_pos[None, :] <= query_pos[:, None]) & (
                key_doc[None, :] == query_doc[:, None]
            )
            scores = (
                jnp.einsum("qhd,khd->hqk", query_tile, key_tile, preferred_element_type=jnp.float32)
                * scale
            )
            return absorb(state, scores, allowed, value_tile)

        start_state = (
            jnp.full((items, span), NEGATIVE, jnp.float32),
            jnp.zeros((items, span), jnp.float32),
            jnp.zeros((items, span, HEAD_WIDTH), jnp.float32),
        )
        final_max, final_sum, final_acc = lax.fori_loop(
            first_span, number + 1, key_span, start_state
        )
        return (final_acc / final_sum[..., None]).transpose(1, 0, 2).astype(jnp.bfloat16)

    tiles = lax.map(query_span, jnp.arange(spans, dtype=jnp.int32))
    return tiles.reshape(stream_len, items, HEAD_WIDTH)


def on_device(queries, keys, values, doc_lengths):
    n_ranks = lax.axis_size("cp")
    n_streams = queries.shape[0]
    rows_per = queries.shape[1]
    group_count = QUERY_HEADS // KEY_VALUE_HEADS
    per_rank = QUERY_HEADS // n_ranks
    stream_id = lax.axis_index("grp")
    lengths_row = lax.dynamic_index_in_dim(doc_lengths, stream_id, 0, keepdims=False)
    ends = jnp.cumsum(lengths_row)

    def by_heads(array):
        shaped = array.reshape(n_streams, rows_per, n_ranks, per_rank, HEAD_WIDTH)
        return shaped.transpose(0, 2, 1, 3, 4).reshape(
            n_streams * n_ranks, rows_per, per_rank, HEAD_WIDTH
        )

    key_wide = jnp.repeat(
        keys.reshape(n_streams, rows_per, KEY_VALUE_HEADS, HEAD_WIDTH), group_count, axis=2
    )
    value_wide = jnp.repeat(
        values.reshape(n_streams, rows_per, KEY_VALUE_HEADS, HEAD_WIDTH), group_count, axis=2
    )
    query_split = by_heads(queries)
    key_divided_rows = by_heads(key_wide)
    value_divided_rows = by_heads(value_wide)
    query_part = lax.all_to_all(query_split, ("grp", "cp"), split_axis=0, concat_axis=1, tiled=True)
    key_portion = lax.all_to_all(
        key_divided_rows, ("grp", "cp"), split_axis=0, concat_axis=1, tiled=True
    )
    value_portion = lax.all_to_all(
        value_divided_rows, ("grp", "cp"), split_axis=0, concat_axis=1, tiled=True
    )
    outcome = attend_stream(query_part[0], key_portion[0], value_portion[0], ends)
    head_output = outcome[None]
    returned = lax.all_to_all(head_output, ("grp", "cp"), split_axis=1, concat_axis=0, tiled=True)
    shaped = returned.reshape(n_streams, n_ranks, rows_per, per_rank, HEAD_WIDTH).transpose(
        0, 2, 1, 3, 4
    )
    return shaped.reshape(n_streams, rows_per, QUERY_HEADS * HEAD_WIDTH)


def solution(mesh):
    n_grp, n_cp = mesh.shape["grp"], mesh.shape["cp"]
    placed = (
        P(None, ("grp", "cp"), None),
        P(None, ("grp", "cp"), None),
        P(None, ("grp", "cp"), None),
        P(),
    )

    def run(queries, keys, values, doc_lengths):
        if window_fits(n_grp, n_cp, queries, keys):
            plan = functools.partial(by_window, n_grp, n_cp)
        else:
            plan = on_device
        return jax.shard_map(
            plan,
            mesh=mesh,
            in_specs=placed,
            out_specs=P(None, ("grp", "cp"), None),
            check_vma=False,
        )(queries, keys, values, doc_lengths)

    return run
```

```python
import functools

import jax
import jax.numpy as jnp
from jax import lax
from jax.experimental import pallas as pl
from jax.experimental.pallas import tpu as pltpu
from jax.sharding import PartitionSpec as P

MESH = pl.DeviceIdType.MESH
PARTS = 4
MOVED = 2
BLOCK = 32
OFF = 2
WINDOW_BYTES = 40 * 2**20

QUERY_HEADS = 32
KEY_VALUE_HEADS = 8
HEAD_WIDTH = 128
NEGATIVE = -1e30
LOG2_E = 1.4426950408889634


def window_kernel(
    n_grp,
    n_cp,
    streams,
    q_ref,
    k_ref,
    v_ref,
    len_ref,
    o_ref,
    kv,
    q_buf,
    o_buf,
    bias,
    scores_buf,
    weights_buf,
    inverse_buf,
    local_sem,
    send_sem,
    recv_sem,
):
    grp, cp = lax.axis_index("grp"), lax.axis_index("cp")
    z, core = cp // 2, cp % 2
    nz = n_cp // 2
    last = nz - 1
    chunks = streams * PARTS
    rows = k_ref.shape[1]
    part = k_ref.shape[2] // PARTS
    heads = part // HEAD_WIDTH
    group = QUERY_HEADS // KEY_VALUE_HEADS
    wide = part * group
    partner = (grp, z * 2 + 1 - core)
    up = (grp, cp + 2)
    down = (grp, cp - 2)
    next_line = ((grp + 1) % n_grp, cp)
    prev_line = ((grp + n_grp - 1) % n_grp, cp)
    fwd_row, hop_row, bwd_row, mate_row = 0, nz - 1, nz - 2, 2 * nz - 1
    far_row, ahead_row, edge_row, ask_row, answer_row = (3 * nz + i for i in range(5))
    ask_slot, answer_slot = n_cp + 2 * OFF + 1, n_cp + 2 * OFF + 2
    at_end = (z == 0) | (z == last)
    helper = (z == 1) | (z == last - 1)

    def moved(ch):
        return ch % MOVED == 0

    def normal(ch):
        return jnp.logical_not(moved(ch) & at_end)

    def local(ch, which):
        source = (k_ref, v_ref)[which]
        cols = pl.ds(pl.multiple_of((ch % PARTS) * part, part), part)
        return pltpu.make_async_copy(
            source.at[ch // PARTS, :, cols],
            kv.at[OFF, ch, :, pl.ds(which * part, part)],
            local_sem.at[which, ch],
        )

    def own_columns(ch):
        return ch // PARTS, slice(None), pl.ds(pl.multiple_of((ch % PARTS) * wide, wide), wide)

    def query_copy(ch):
        return pltpu.make_async_copy(q_ref.at[own_columns(ch)], q_buf.at[ch], local_sem.at[2, ch])

    def result_copy(ch):
        return pltpu.make_async_copy(o_buf.at[ch], o_ref.at[own_columns(ch)], local_sem.at[3, ch])

    def remote(source, target, ch, row, device):
        return pltpu.make_async_remote_copy(
            src_ref=kv.at[OFF + source, ch],
            dst_ref=kv.at[OFF + target, ch],
            send_sem=send_sem.at[row, ch],
            recv_sem=recv_sem.at[OFF + target, ch],
            device_id=device,
            device_id_type=MESH,
        )

    def arrived(slot, ch):
        remote(slot, slot, ch, 0, partner).wait_recv()

    def ask(ch, device):
        return pltpu.make_async_remote_copy(
            src_ref=q_buf.at[ch],
            dst_ref=q_buf.at[chunks + ch // MOVED],
            send_sem=send_sem.at[ask_row, ch],
            recv_sem=recv_sem.at[ask_slot, ch],
            device_id=device,
            device_id_type=MESH,
        )

    def answer(ch, device):
        return pltpu.make_async_remote_copy(
            src_ref=o_buf.at[chunks + ch // MOVED],
            dst_ref=o_buf.at[ch],
            send_sem=send_sem.at[answer_row, ch],
            recv_sem=recv_sem.at[answer_slot, ch],
            device_id=device,
            device_id_type=MESH,
        )

    @pl.loop(0, chunks)
    def _(ch):
        local(ch, 0).start()
        local(ch, 1).start()

    @pl.loop(0, chunks)
    def _(ch):
        query_copy(ch).start()

    barrier = pltpu.get_barrier_semaphore()

    def greet(device):
        pl.semaphore_signal(barrier, inc=1, device_id=device, device_id_type=MESH)

    greet(partner)
    greet(next_line)
    greet(prev_line)

    @pl.when(z < last)
    def _():
        greet(up)

    @pl.when(z > 0)
    def _():
        greet(down)

    pl.semaphore_wait(barrier, jnp.where(at_end, 4, 5))

    def to_partner(d, ch):
        if d < nz:

            @pl.when(core == 0)
            def _():
                remote(2 * d, 2 * d + 1, ch, mate_row + d, partner).start()

        if d > 0:

            @pl.when(core == 1)
            def _():
                remote(2 * d, 2 * d - 1, ch, mate_row + d, partner).start()

    def attend(ch, q_at, shift):
        stream = ch // PARTS
        base = (grp * n_cp + cp - shift) * rows
        row = lax.broadcasted_iota(jnp.int32, (rows, rows), 0)
        lane = lax.broadcasted_iota(jnp.int32, (rows, rows), 1)
        first = jnp.zeros((rows, rows), jnp.int32)
        end = jnp.int32(0)
        for doc in range(len_ref.shape[1]):
            end = end + len_ref[stream, doc]
            first = jnp.maximum(first, jnp.where(row + base >= end, end, 0))
        for r in range(n_cp + 1):
            allowed = lane + (base - r * rows) >= first
            if r == 0:
                allowed = allowed & (lane <= row)
            bias[:, r * rows : (r + 1) * rows] = jnp.where(allowed, 0.0, NEGATIVE)

        slots = [OFF + shift + r for r in range(n_cp + 1)]

        def q_cols(head, j):
            at = (head * group + j) * HEAD_WIDTH
            return slice(at, at + HEAD_WIDTH)

        for head in range(heads):
            k_cols = slice(head * HEAD_WIDTH, (head + 1) * HEAD_WIDTH)
            scores_buf[head] = lax.dot_general(
                jnp.concatenate([q_buf[q_at, :, q_cols(head, j)] for j in range(group)], axis=0),
                jnp.concatenate([kv[slot, ch, :, k_cols] for slot in slots], axis=0),
                (((1,), (1,)), ((), ())),
                preferred_element_type=jnp.float32,
            )

        def normalise(i, carry):
            at = pl.ds(pl.multiple_of(i * BLOCK, BLOCK), BLOCK)
            token = pl.ds(pl.multiple_of(i % (rows // BLOCK) * BLOCK, BLOCK), BLOCK)
            mask = bias[token, :]
            for head in range(heads):
                scores = scores_buf[head, at, :] + mask
                largest = jnp.max(scores, axis=1, keepdims=True)
                probs = jnp.exp2((scores - largest) * (HEAD_WIDTH**-0.5 * LOG2_E))
                total = jnp.sum(probs, axis=1, keepdims=True)
                weights_buf[head, at, :] = probs.astype(jnp.bfloat16)
                inverse_buf[head, at, :] = jnp.broadcast_to(1.0 / total, (BLOCK, HEAD_WIDTH))
            return carry

        lax.fori_loop(0, group * rows // BLOCK, normalise, 0, unroll=2)

        for head in range(heads):
            v_cols = slice(part + head * HEAD_WIDTH, part + (head + 1) * HEAD_WIDTH)
            summed = jnp.dot(
                weights_buf[head],
                jnp.concatenate([kv[slot, ch, :, v_cols] for slot in slots], axis=0),
                preferred_element_type=jnp.float32,
            )
            result = (summed * inverse_buf[head]).astype(o_buf.dtype)
            for j in range(group):
                o_buf[q_at, :, q_cols(head, j)] = result[j * rows : (j + 1) * rows]

    lag = jnp.maximum(2 * (nz - z), 2 * z)

    @pl.loop(0, chunks + 2 * nz)
    def _(t):
        @pl.when(t < chunks)
        def _():
            local(t, 0).wait()
            local(t, 1).wait()

            @pl.when(normal(t))
            def _():
                remote(0, 2 * nz, t, hop_row, next_line).start()

            @pl.when((z < last) & (jnp.logical_not(moved(t)) | (z < last - 1)))
            def _():
                remote(0, 2, t, fwd_row, up).start()

            @pl.when(moved(t) & (z == last))
            def _():
                remote(0, -2, t, ahead_row, down).start()

            @pl.when(normal(t))
            def _():
                to_partner(0, t)

            @pl.when(moved(t) & (z == last - 1) & (core == 1))
            def _():
                remote(0, -1, t, edge_row, partner).start()

        for d in range(nz, 0, -1):
            ch = t - 2 * (nz + 1 - d)

            @pl.when((ch >= 0) & (ch < chunks) & (z < d) & normal(ch))
            def _():
                arrived(2 * d, ch)
                if d > 1:

                    @pl.when((z > 0) & (jnp.logical_not(moved(ch)) | (z > 1)))
                    def _():
                        remote(2 * d, 2 * d - 2, ch, bwd_row + d, down).start()

                to_partner(d, ch)
                if d == nz:

                    @pl.when(moved(ch) & (z == 1) & (core == 0))
                    def _():
                        remote(2 * nz, 2 * nz + 1, ch, edge_row, partner).start()

        for d in range(1, nz):
            ch = t - 2 * d

            @pl.when((ch >= 0) & (ch < chunks) & (z >= d) & normal(ch))
            def _():
                arrived(2 * d, ch)
                if d < nz - 1:

                    @pl.when((z < last) & (jnp.logical_not(moved(ch)) | (z < last - 1)))
                    def _():
                        remote(2 * d, 2 * d + 2, ch, fwd_row + d, up).start()

                to_partner(d, ch)
                if d == 1:

                    @pl.when(moved(ch) & (z == 1))
                    def _():
                        remote(2, 2 * nz + 2, ch, far_row, next_line).start()

        before = t - 1

        @pl.when((before >= 0) & (before < chunks) & moved(before))
        def _():
            @pl.when(at_end)
            def _():
                query_copy(before).wait()

            @pl.when(z == 0)
            def _():
                ask(before, up).start()

            @pl.when(z == last)
            def _():
                ask(before, down).start()

        earlier = t - 2

        @pl.when((earlier >= 0) & (earlier < chunks) & moved(earlier) & (z == last - 1))
        def _():
            arrived(-2, earlier)
            remote(-2, 2 * nz - 2, earlier, far_row, next_line).start()

            @pl.when(core == 0)
            def _():
                remote(-2, -1, earlier, edge_row, partner).start()

        earlier = t - 4

        @pl.when((earlier >= 0) & (earlier < chunks) & moved(earlier) & (z == 1))
        def _():
            arrived(2 * nz + 2, earlier)

            @pl.when(core == 1)
            def _():
                remote(2 * nz + 2, 2 * nz + 1, earlier, edge_row, partner).start()

        ch = t - lag

        @pl.when((ch >= 0) & (ch < chunks) & normal(ch))
        def _():
            for d in range(nz):
                arrived(2 * d + 1, ch)
            query_copy(ch).wait()
            helps = helper & moved(ch)

            @pl.when(helps)
            def _():
                ask(ch, partner).wait_recv()

                @pl.when(z == 1)
                def _():
                    arrived(2 * nz + 1, ch)

                @pl.when(z == last - 1)
                def _():
                    arrived(-1, ch)

            @pl.loop(jnp.where(helps, 0, 1), 2)
            def _(own):
                other = 1 - own
                attend(
                    ch,
                    other * (chunks + ch // MOVED) + own * ch,
                    other * jnp.where(z == 1, 2, -2),
                )

                @pl.when(other == 1)
                def _():
                    @pl.when(z == 1)
                    def _():
                        answer(ch, down).start()

                    @pl.when(z == last - 1)
                    def _():
                        answer(ch, up).start()

            result_copy(ch).start()

    @pl.loop(0, chunks)
    def _(ch):
        def sent(row):
            remote(0, 1, ch, row, partner).wait_send()

        @pl.when(moved(ch) & at_end)
        def _():
            answer(ch, partner).wait_recv()
            result_copy(ch).start()
            ask(ch, partner).wait_send()

        result_copy(ch).wait()

        @pl.when(moved(ch) & helper)
        def _():
            sent(far_row)
            sent(edge_row)
            answer(ch, partner).wait_send()

        @pl.when(moved(ch) & (z == last))
        def _():
            sent(ahead_row)

        for d in range(nz - 1):

            @pl.when((z >= d) & (z < last) & (jnp.logical_not(moved(ch)) | (z < last - 1)))
            def _():
                sent(fwd_row + d)

        for d in range(2, nz + 1):

            @pl.when((z < d) & (z > 0) & (jnp.logical_not(moved(ch)) | ((z > 1) & (z < last))))
            def _():
                sent(bwd_row + d)

        @pl.when(normal(ch))
        def _():
            sent(hop_row)
            for d in range(nz + 1):
                if d == 0:

                    @pl.when(core == 0)
                    def _():
                        sent(mate_row)

                elif d == nz:

                    @pl.when(core == 1)
                    def _():
                        sent(mate_row + nz)

                else:
                    sent(mate_row + d)


def by_window(n_grp, n_cp, queries, keys, values, doc_lengths):
    streams, rows, _ = queries.shape
    chunks = streams * PARTS
    width = 2 * keys.shape[2] // PARTS
    window = (n_cp + 1) * rows
    nz = n_cp // 2
    pairs = streams * QUERY_HEADS * rows * window
    heads = KEY_VALUE_HEADS // PARTS
    stacked = rows * QUERY_HEADS // KEY_VALUE_HEADS
    held = (chunks + chunks // MOVED, rows, queries.shape[2] // PARTS)
    return pl.pallas_call(
        functools.partial(window_kernel, n_grp, n_cp, streams),
        out_shape=jax.ShapeDtypeStruct(queries.shape, queries.dtype),
        in_specs=[
            pl.BlockSpec(memory_space=pl.ANY),
            pl.BlockSpec(memory_space=pl.ANY),
            pl.BlockSpec(memory_space=pl.ANY),
            pl.BlockSpec(memory_space=pltpu.SMEM),
        ],
        out_specs=pl.BlockSpec(memory_space=pl.ANY),
        scratch_shapes=[
            pltpu.VMEM((n_cp + 1 + 2 * OFF, chunks, rows, width), keys.dtype),
            pltpu.VMEM(held, queries.dtype),
            pltpu.VMEM(held, queries.dtype),
            pltpu.VMEM((rows, window), jnp.float32),
            pltpu.VMEM((heads, stacked, window), jnp.float32),
            pltpu.VMEM((heads, stacked, window), jnp.bfloat16),
            pltpu.VMEM((heads, stacked, HEAD_WIDTH), jnp.float32),
            pltpu.SemaphoreType.DMA((4, chunks)),
            pltpu.SemaphoreType.DMA((3 * nz + 5, chunks)),
            pltpu.SemaphoreType.DMA((n_cp + 3 + 2 * OFF, chunks)),
        ],
        cost_estimate=pl.CostEstimate(
            flops=4 * pairs * HEAD_WIDTH, bytes_accessed=5 * queries.size, transcendentals=pairs
        ),
        compiler_params=pltpu.CompilerParams(
            collective_id=0, has_side_effects=True, vmem_limit_bytes=56 * 2**20
        ),
        name="window_attention",
    )(queries, keys, values, doc_lengths)


def window_fits(n_grp, n_cp, queries, keys):
    line = 2 * keys.shape[0] * keys.shape[1] // n_grp * keys.shape[2] * keys.dtype.itemsize
    return n_cp % 2 == 0 and n_cp >= 8 and n_grp >= 3 and line <= WINDOW_BYTES


def doc_of(positions, ends):
    return jnp.sum((positions[:, None] >= ends[None, :]).astype(jnp.int32), axis=1)


def doc_first(positions, ends):
    return jnp.max(jnp.where(ends[None, :] <= positions[:, None], ends[None, :], 0), axis=1)


def absorb(state, scores, allowed, value_portion):
    running_max, running_sum, running_acc = state
    scores = jnp.where(allowed, scores, NEGATIVE)
    new_max = jnp.maximum(running_max, jnp.max(scores, axis=-1))
    factor = jnp.exp(running_max - new_max)
    probs = jnp.where(allowed, jnp.exp(scores - new_max[..., None]), 0.0)
    new_sum = running_sum * factor + jnp.sum(probs, axis=-1)
    product = jnp.einsum(
        "hqk,khd->hqd",
        probs.astype(jnp.bfloat16),
        value_portion,
        preferred_element_type=jnp.float32,
    )
    return (new_max, new_sum, running_acc * factor[..., None] + product)


def attend_stream(query_seq, key_seq, value_seq, ends):
    stream_len = query_seq.shape[0]
    items = query_seq.shape[1]
    scale = HEAD_WIDTH ** (-0.5)
    positions = jnp.arange(stream_len, dtype=jnp.int32)
    all_docs = doc_of(positions, ends)
    all_firsts = doc_first(positions, ends)
    span = min(512, stream_len)
    spans = stream_len // span

    def query_span(number):
        begin = number * span
        query_tile = lax.dynamic_slice_in_dim(query_seq, begin, span, 0)
        query_pos = lax.dynamic_slice_in_dim(positions, begin, span, 0)
        query_doc = lax.dynamic_slice_in_dim(all_docs, begin, span, 0)
        first_span = lax.dynamic_index_in_dim(all_firsts, begin, 0, keepdims=False) // span

        def key_span(other, state):
            offset = other * span
            key_tile = lax.dynamic_slice_in_dim(key_seq, offset, span, 0)
            value_tile = lax.dynamic_slice_in_dim(value_seq, offset, span, 0)
            key_pos = lax.dynamic_slice_in_dim(positions, offset, span, 0)
            key_doc = lax.dynamic_slice_in_dim(all_docs, offset, span, 0)
            allowed = (key_pos[None, :] <= query_pos[:, None]) & (
                key_doc[None, :] == query_doc[:, None]
            )
            scores = (
                jnp.einsum("qhd,khd->hqk", query_tile, key_tile, preferred_element_type=jnp.float32)
                * scale
            )
            return absorb(state, scores, allowed, value_tile)

        start_state = (
            jnp.full((items, span), NEGATIVE, jnp.float32),
            jnp.zeros((items, span), jnp.float32),
            jnp.zeros((items, span, HEAD_WIDTH), jnp.float32),
        )
        final_max, final_sum, final_acc = lax.fori_loop(
            first_span, number + 1, key_span, start_state
        )
        return (final_acc / final_sum[..., None]).transpose(1, 0, 2).astype(jnp.bfloat16)

    tiles = lax.map(query_span, jnp.arange(spans, dtype=jnp.int32))
    return tiles.reshape(stream_len, items, HEAD_WIDTH)


def on_device(queries, keys, values, doc_lengths):
    n_ranks = lax.axis_size("cp")
    n_streams = queries.shape[0]
    rows_per = queries.shape[1]
    group_count = QUERY_HEADS // KEY_VALUE_HEADS
    per_rank = QUERY_HEADS // n_ranks
    stream_id = lax.axis_index("grp")
    lengths_row = lax.dynamic_index_in_dim(doc_lengths, stream_id, 0, keepdims=False)
    ends = jnp.cumsum(lengths_row)

    def by_heads(array):
        shaped = array.reshape(n_streams, rows_per, n_ranks, per_rank, HEAD_WIDTH)
        return shaped.transpose(0, 2, 1, 3, 4).reshape(
            n_streams * n_ranks, rows_per, per_rank, HEAD_WIDTH
        )

    key_wide = jnp.repeat(
        keys.reshape(n_streams, rows_per, KEY_VALUE_HEADS, HEAD_WIDTH), group_count, axis=2
    )
    value_wide = jnp.repeat(
        values.reshape(n_streams, rows_per, KEY_VALUE_HEADS, HEAD_WIDTH), group_count, axis=2
    )
    query_split = by_heads(queries)
    key_divided_rows = by_heads(key_wide)
    value_divided_rows = by_heads(value_wide)
    query_part = lax.all_to_all(query_split, ("grp", "cp"), split_axis=0, concat_axis=1, tiled=True)
    key_portion = lax.all_to_all(
        key_divided_rows, ("grp", "cp"), split_axis=0, concat_axis=1, tiled=True
    )
    value_portion = lax.all_to_all(
        value_divided_rows, ("grp", "cp"), split_axis=0, concat_axis=1, tiled=True
    )
    outcome = attend_stream(query_part[0], key_portion[0], value_portion[0], ends)
    head_output = outcome[None]
    returned = lax.all_to_all(head_output, ("grp", "cp"), split_axis=1, concat_axis=0, tiled=True)
    shaped = returned.reshape(n_streams, n_ranks, rows_per, per_rank, HEAD_WIDTH).transpose(
        0, 2, 1, 3, 4
    )
    return shaped.reshape(n_streams, rows_per, QUERY_HEADS * HEAD_WIDTH)


def solution(mesh):
    n_grp, n_cp = mesh.shape["grp"], mesh.shape["cp"]
    placed = (
        P(None, ("grp", "cp"), None),
        P(None, ("grp", "cp"), None),
        P(None, ("grp", "cp"), None),
        P(),
    )

    def run(queries, keys, values, doc_lengths):
        if window_fits(n_grp, n_cp, queries, keys):
            plan = functools.partial(by_window, n_grp, n_cp)
        else:
            plan = on_device
        return jax.shard_map(
            plan,
            mesh=mesh,
            in_specs=placed,
            out_specs=P(None, ("grp", "cp"), None),
            check_vma=False,
        )(queries, keys, values, doc_lengths)

    return run
```
